256 devices in a mesh: grp: 4 (over x_lo, core), blk: 64 (over x_hi, z, y).
Axes of the slice: x: 4 (x_hi: 2, x_lo: 2; x = x_hi * 2 + x_lo), y: 4, z: 8, core: 2. Of those that a mesh axis runs over, the one named last changes fastest.
Arguments:
- masses: bfloat16 [64, 2, 256, 256], P('blk'), may hold values from -3 to 3
- spins: int32 [64, 256], P('blk'), may hold values from 0 to 1
- shift_table: int32 [256, 256], P('blk'), may hold values from 0 to 255, as said below
- flip_table: int32 [256, 256], P('blk'), may hold values from 0 to 255, as said below
- ph_in: float32 [2, 256, 256, 256], P(None, 'blk', 'grp'), may hold values from -6 to 6
- pp_in: float32 [2, 256, 256, 256], P(None, 'blk', 'grp'), may hold values from -6 to 6
Outputs:
- ph_out: float32 [2, 256, 256, 256], P(None, 'blk', 'grp')
- pp_out: float32 [2, 256, 256, 256], P(None, 'blk', 'grp')
The draws below stay inside these ranges and needn't reach their ends.
Inputs may be any that keep to these rules, and one draw needn't show every extreme that they name: Row t of shift_table maps w * 16 + k to ((w + n_t) mod 16) * 16 + (k + q_t) mod 16 for some integers n_t, q_t of the transfer; every row is a permutation. Row t of flip_table maps w * 16 + k to ((n_t - w - 1) mod 16) * 16 + (q_t - k) mod 16 with the same n_t, q_t as shift_table's row t.
All inputs are finite; a program needn't handle non-finite values.
Results may differ from the reference program's by a relative error of at most 0.0064.
Values may be sent and summed in bfloat16 or wider, within the bound.
No kernel may reach another device: no remote copies, remote signals or barrier semaphores. Data moves between devices by JAX's collectives and lax.ppermute only.
A program may use at most 128 MiB of HBM per device.

```python
import math
import jax
import jax.numpy as jnp
from jax import lax

NW = 16
NK = 16
ORDER = 256
WALK_DEV = 1
TR_DEV = 4
WALKERS = 64
TRANS = 256
SHIFTS = 8
N_BLK = 64


def table_moves(key):
    momentum_move = jax.random.randint(jax.random.fold_in(key, 71), (TRANS,), 0, NK)
    frequency_move = jax.random.randint(jax.random.fold_in(key, 72), (TRANS,), 0, NW)
    return (momentum_move, frequency_move)


def draw_shift_table(key, part):
    momentum_move, frequency_move = table_moves(key)
    index = jnp.arange(NW * NK, dtype=jnp.int32)
    frequency = index // NK
    momentum = index % NK
    result = (frequency[None, :] + frequency_move[:, None]) % NW * NK + (momentum[None, :] + momentum_move[:, None]) % NK
    return result.astype(jnp.int32)


def draw_flip_table(key, part):
    momentum_move, frequency_move = table_moves(key)
    index = jnp.arange(NW * NK, dtype=jnp.int32)
    frequency = index // NK
    momentum = index % NK
    result = (frequency_move[:, None] - frequency[None, :] - 1) % NW * NK + (momentum_move[:, None] - momentum[None, :]) % NK
    return result.astype(jnp.int32)


def plant(values, own_key, smallest, top_value):
    extent = values.shape
    spot = [jax.random.randint(jax.random.fold_in(own_key, axis), (), 0, extent[axis]) for axis in range(len(extent))]
    values = values.at[tuple(spot)].set(smallest)
    longest = extent.index(max(extent))
    spot[longest] = (spot[longest] + 1) % extent[longest]
    return values.at[tuple(spot)].set(top_value)


def steps_of(key, shape, cuts, least, largest):
    level, own = 1.0, jax.random.fold_in(key, 6)
    for position, blocks in cuts:
        draws = jnp.exp(jax.random.uniform(jax.random.fold_in(own, position), (blocks,), jnp.float32, least / len(cuts), largest / len(cuts)))
        level = level * jnp.repeat(draws, shape[position] // blocks).reshape([-1 if axis == position else 1 for axis in range(len(shape))])
    return level


def noise(rng, extent, width, bound, cuts=(), kind=jnp.bfloat16):
    array = width * jax.random.normal(rng, extent, jnp.float32)
    if cuts:
        array = array * steps_of(rng, extent, cuts, -0.22, 0.18)
    return jnp.clip(array, -bound, bound).astype(kind)


def setup_inputs(seed: int = 0) -> dict:
    key_of = jax.random.split(jax.random.key(seed), 7)
    return {
        "masses": noise(key_of[0], (WALKERS, 2, ORDER, ORDER), 0.5, 3.0, ((0, 64),)),
        "spins": plant(jax.random.randint(key_of[1], (WALKERS, ORDER), 0, 2), jax.random.fold_in(key_of[1], 1), 0, 1).astype(jnp.int32),
        "shift_table": draw_shift_table(jax.random.fold_in(key_of[6], 71), 0),
        "flip_table": draw_flip_table(jax.random.fold_in(key_of[6], 71), 0),
        "ph_in": noise(key_of[4], (2, TRANS, ORDER, ORDER), 1.0, 6.0, ((1, 64), (2, 4)), jnp.float32),
        "pp_in": noise(key_of[5], (2, TRANS, ORDER, ORDER), 1.0, 6.0, ((1, 64), (2, 4)), jnp.float32),
    }


COUPLING = 0.5

def dft_tables():
    index = jnp.arange(NW * NK, dtype=jnp.int32)
    frequency = index // NK
    momentum = index % NK
    numerator = ((2 * frequency[:, None] + 1) * frequency[None, :] * NK - 2 * momentum[:, None] * momentum[None, :] * NW) % (2 * NW * NK)
    phase = numerator.astype(jnp.float32) * (math.pi / (NW * NK))
    norm_scale = 1.0 / math.sqrt(NW * NK)
    return ((jnp.cos(phase) * norm_scale).astype(jnp.bfloat16), (jnp.sin(phase) * norm_scale).astype(jnp.bfloat16))

def build(masses, spins, real_table, imag_table):
    signed = (2 * spins - 1).astype(jnp.float32)
    factors = jnp.stack([jnp.exp(COUPLING * signed), jnp.exp(-COUPLING * signed)], 1)
    scaled = (masses.astype(jnp.float32) * factors[:, :, None, :]).astype(jnp.bfloat16).astype(jnp.float32)
    first_real = jnp.einsum('ri,wsij->wsrj', real_table.astype(jnp.float32), scaled).astype(jnp.bfloat16)
    first_imag = jnp.einsum('ri,wsij->wsrj', imag_table.astype(jnp.float32), scaled).astype(jnp.bfloat16)
    joined = jnp.concatenate([first_real, first_imag], -1).astype(jnp.float32)
    big_table = jnp.concatenate([jnp.concatenate([real_table.T, -imag_table.T], 1), jnp.concatenate([imag_table.T, real_table.T], 1)], 0).astype(jnp.float32)
    second = jnp.einsum('wsri,ij->wsrj', joined, big_table)
    order = real_table.shape[1]
    return jnp.stack([second[..., :order], second[..., order:]], 2).astype(jnp.bfloat16)

def reference(masses, spins, shift_table, flip_table, ph_in, pp_in):
    real_table, imag_table = dft_tables()
    propagator = build(masses, spins, real_table, imag_table)

    def one_block(block, totals):
        ph_total, pp_total = totals
        homes = (block - jnp.arange(SHIFTS + 1, dtype=jnp.int32)) % N_BLK
        walker_ids = (homes[:, None] * WALK_DEV + jnp.arange(WALK_DEV, dtype=jnp.int32)[None, :]).reshape(-1)
        props = propagator[walker_ids].astype(jnp.float32)
        begin = (block * TR_DEV).astype(jnp.int32)
        shifts = lax.dynamic_slice_in_dim(shift_table, begin, TR_DEV, 0)
        flips = lax.dynamic_slice_in_dim(flip_table, begin, TR_DEV, 0)
        mirrored = jnp.swapaxes(props, 3, 4)[:, :, :, None]
        moved = props[:, :, :, shifts[:, :, None], shifts[:, None, :]]
        ph_real = lax.optimization_barrier(jnp.sum(mirrored[:, :, 0] * moved[:, :, 0] - mirrored[:, :, 1] * moved[:, :, 1], axis=(0, 1)))
        ph_imag = lax.optimization_barrier(jnp.sum(mirrored[:, :, 0] * moved[:, :, 1] + mirrored[:, :, 1] * moved[:, :, 0], axis=(0, 1)))
        upper = props[:, 0][:, :, None]
        lowered = props[:, 1][:, :, flips[:, :, None], flips[:, None, :]]
        pp_real = lax.optimization_barrier(jnp.sum(upper[:, 0] * lowered[:, 0] - upper[:, 1] * lowered[:, 1], axis=0))
        pp_imag = lax.optimization_barrier(jnp.sum(upper[:, 0] * lowered[:, 1] + upper[:, 1] * lowered[:, 0], axis=0))
        ph_old = lax.dynamic_slice_in_dim(ph_total, begin, TR_DEV, 1)
        pp_old = lax.dynamic_slice_in_dim(pp_total, begin, TR_DEV, 1)
        ph_total = lax.dynamic_update_slice_in_dim(ph_total, ph_old + jnp.stack([ph_real, ph_imag]), begin, 1)
        pp_total = lax.dynamic_update_slice_in_dim(pp_total, pp_old + jnp.stack([pp_real, pp_imag]), begin, 1)
        return (ph_total, pp_total)
    ph_out, pp_out = lax.fori_loop(0, N_BLK, one_block, (ph_in, pp_in))
    return (ph_out, pp_out)
```

```python
import functools
import math

import jax
import jax.numpy as jnp
from jax import lax
from jax.experimental import pallas as pl
from jax.experimental.pallas import tpu as pltpu
from jax.sharding import PartitionSpec as P

NK = 16
ORDER = 256
BAND = 64
TRANS = 4
COUPLING = 0.5
BF = jnp.bfloat16
F32 = jnp.float32
MIB = 1 << 20


def wave(freq, mom, tau, site):
    turns = ((2 * freq + 1) * tau - 2 * mom * site) & 31
    phase = turns.astype(F32) * (math.pi / 16.0)
    return (jnp.cos(phase) * 0.0625).astype(BF), (jnp.sin(phase) * 0.0625).astype(BF)


def table_kernel(place_ref, shift_ref, flip_ref, cols_ref, rows_ref):
    square = (ORDER, ORDER)
    sub = lax.broadcasted_iota(jnp.int32, square, 0)
    lane = lax.broadcasted_iota(jnp.int32, square, 1)
    re, im = wave(lane >> 4, lane & 15, sub >> 4, sub & 15)
    cols_ref[2 * TRANS, :ORDER] = re
    cols_ref[2 * TRANS, ORDER:] = im
    re, im = wave(sub >> 4, sub & 15, lane >> 4, lane & 15)
    base = jnp.concatenate([re, im], 1)
    band_row = lax.broadcasted_iota(jnp.int32, (BAND, ORDER), 0) + place_ref[0] * BAND
    band_lane = lax.broadcasted_iota(jnp.int32, (BAND, ORDER), 1)

    def put_rows(slot, target):
        pick = jnp.where(band_lane == target, 1.0, 0.0).astype(BF)
        out = jnp.dot(pick, base, preferred_element_type=F32).astype(BF)
        rows_ref[2 * BAND * slot : 2 * BAND * slot + BAND] = out[:, :ORDER]
        rows_ref[2 * BAND * slot + BAND : 2 * BAND * (slot + 1)] = out[:, ORDER:]

    def put_cols(slot, target):
        pick = jnp.where(sub == target, 1.0, 0.0).astype(BF)
        cols_ref[slot] = jnp.dot(cols_ref[2 * TRANS], pick, preferred_element_type=F32).astype(BF)

    put_rows(0, band_row)
    for t in range(TRANS):
        freq, mom = shift_ref[t, 0] >> 4, shift_ref[t, 0] & 15

        def moved(i, freq=freq, mom=mom):
            return ((((i >> 4) + freq) & 15) << 4) + (((i & 15) + mom) & 15)

        put_rows(1 + t, moved(band_row))
        put_cols(t, moved(lane))
        freq, mom = flip_ref[t, 0] >> 4, flip_ref[t, 0] & 15

        def turned(i, freq=freq, mom=mom):
            return (((freq - (i >> 4)) & 15) << 4) + ((mom - (i & 15)) & 15)

        put_rows(1 + TRANS + t, turned(band_row))
        put_cols(TRANS + t, turned(lane))


def tables(place, shift, flip):
    return pl.pallas_call(
        table_kernel,
        out_shape=(
            jax.ShapeDtypeStruct((2 * TRANS + 1, 2 * ORDER, ORDER), BF),
            jax.ShapeDtypeStruct(((2 * TRANS + 1) * 2 * BAND, ORDER), BF),
        ),
        in_specs=[pl.BlockSpec(memory_space=pltpu.SMEM)] * 3,
        out_specs=(pl.BlockSpec(memory_space=pltpu.VMEM),) * 2,
        cost_estimate=pl.CostEstimate(flops=2 * 10**9, bytes_accessed=3 * 10**6, transcendentals=0),
        compiler_params=pltpu.CompilerParams(vmem_limit_bytes=20 * MIB),
        name="tables",
    )(place, shift, flip)


def paired(re, im):
    return jnp.concatenate(
        [jnp.concatenate([re, im], 1), jnp.concatenate([im, -re], 1)], 0
    )


def halves(ref, begin):
    return paired(ref[begin : begin + BAND], ref[begin + BAND : begin + 2 * BAND])


def one_walker(up, down, cols, rows, ph, pp, first_up, first_down, plain):
    step = 2 * BAND
    first_up[...] = jnp.dot(rows[: step * (TRANS + 1)], up, preferred_element_type=F32).astype(BF)
    first_down[...] = jnp.dot(rows[step:], down, preferred_element_type=F32).astype(BF)
    across = (((1,), (1,)), ((), ()))
    turned_up = lax.dot_general(rows[:step], up, across, preferred_element_type=F32).astype(BF)
    turned_down = lax.dot_general(rows[:step], down, across, preferred_element_type=F32).astype(BF)
    left = jnp.concatenate(
        [halves(turned_up, 0), halves(turned_down, 0), halves(first_up, 0)], 0
    )
    plain[...] = jnp.dot(left, cols[2 * TRANS], preferred_element_type=F32)
    for t in range(TRANS):
        left = jnp.concatenate([halves(first_up, step * (1 + t)), halves(first_down, step * t)], 0)
        moved = jnp.dot(left, cols[t], preferred_element_type=F32)
        real, imag = 0.0, 0.0
        for s in range(2):
            nr, ni = plain[step * s : step * s + BAND], plain[step * s + BAND : step * (s + 1)]
            mr, mi = moved[step * s : step * s + BAND], moved[step * s + BAND : step * (s + 1)]
            real = real + (nr * mr + ni * mi)
            imag = imag + (nr * mi - ni * mr)
        ph[0, t] += real
        ph[1, t] += imag
        low = jnp.dot(
            halves(first_down, step * (TRANS + t)), cols[TRANS + t], preferred_element_type=F32
        )
        nr, ni = plain[2 * step : 2 * step + BAND], plain[2 * step + BAND : 3 * step]
        pp[0, t] += nr * low[:BAND] - ni * low[BAND:]
        pp[1, t] += nr * low[BAND:] + ni * low[:BAND]


def absorb_kernel(count, *refs):
    place = refs[0]
    mine, theirs = refs[1 : 1 + count], refs[1 + count : 1 + 2 * count]
    cols, rows, ph_in, pp_in, ph, pp = refs[1 + 2 * count : 7 + 2 * count]
    hold, first_up, first_down, plain, sems = refs[7 + 2 * count :]
    core = place[0] & 1
    for i in range(count):
        pltpu.make_async_copy(mine[i], hold.at[i, core], sems.at[i, 0]).start()
        pltpu.make_async_copy(theirs[i], hold.at[i, 1 - core], sems.at[i, 1]).start()
    ph[...] = ph_in[...]
    pp[...] = pp_in[...]
    for i in range(count):
        pltpu.make_async_copy(mine[i], hold.at[i, core], sems.at[i, 0]).wait()
        pltpu.make_async_copy(theirs[i], hold.at[i, 1 - core], sems.at[i, 1]).wait()

    def step(i, carry):
        one_walker(hold[i, 0], hold[i, 1], cols, rows, ph, pp, first_up, first_down, plain)
        return carry

    lax.fori_loop(0, count, step, 0)


def absorb(place, mine, theirs, cols, rows, ph, pp, fresh):
    count = len(mine)
    return pl.pallas_call(
        functools.partial(absorb_kernel, count),
        out_shape=(jax.ShapeDtypeStruct(ph.shape, F32), jax.ShapeDtypeStruct(pp.shape, F32)),
        in_specs=[pl.BlockSpec(memory_space=pltpu.SMEM)]
        + [pl.BlockSpec(memory_space=pl.ANY)] * (2 * count)
        + [pl.BlockSpec(memory_space=pltpu.VMEM)] * 4,
        out_specs=(pl.BlockSpec(memory_space=pltpu.VMEM),) * 2,
        scratch_shapes=[
            pltpu.VMEM((count, 2, ORDER, ORDER), BF),
            pltpu.VMEM((2 * BAND * (TRANS + 1), ORDER), BF),
            pltpu.VMEM((2 * BAND * 2 * TRANS, ORDER), BF),
            pltpu.VMEM((6 * BAND, ORDER), F32),
            pltpu.SemaphoreType.DMA((count, 2)),
        ],
        input_output_aliases={} if fresh else {3 + 2 * count: 0, 4 + 2 * count: 1},
        cost_estimate=pl.CostEstimate(
            flops=count * 10**9, bytes_accessed=4 * 10**6, transcendentals=0
        ),
        compiler_params=pltpu.CompilerParams(vmem_limit_bytes=24 * MIB),
        name="absorb",
    )(place, *mine, *theirs, cols, rows, ph, pp)


def along_ring(value, steps):
    return lax.ppermute(value, "blk", [(s, (s + steps) % 64) for s in range(64)])


def along_y(value, steps):
    return lax.ppermute(value, "blk", [(s, s // 4 * 4 + (s + steps) % 4) for s in range(64)])


def other_core(value):
    return lax.ppermute(value, "grp", [(s, s ^ 1) for s in range(4)])


def on_device(masses, spins, shift_table, flip_table, ph_in, pp_in):
    grp = lax.axis_index("grp")
    y = lax.axis_index("blk") % 4
    place = grp.reshape(1).astype(jnp.int32)
    signed = (2 * spins[0] - 1).astype(F32)
    core = grp % 2
    signs = jnp.stack([1 - 2 * core, 2 * core - 1]).astype(F32) * COUPLING

    def scaled(spin, sign):
        matrix = lax.dynamic_index_in_dim(masses[0], spin, 0, keepdims=False)
        return (matrix.astype(F32) * jnp.exp(sign * signed)[None, :]).astype(BF)

    own, own_other = scaled(core, signs[0]), scaled(1 - core, signs[1])
    near = along_ring(own, 4)
    far = along_ring(own, 8)
    cols, rows = tables(place, shift_table, flip_table)
    ph, pp = absorb(place, [own], [own_other], cols, rows, ph_in, pp_in, True)
    aside = [along_y(near, d) for d in (1, 3, 2)]
    wrapped = [along_y(jnp.where(y + d >= 4, far, own), d) for d in (1, 3, 2)]
    early = [near, far] + aside
    early_other = [other_core(v) for v in early]
    late_other = [other_core(v) for v in wrapped]
    ph, pp = absorb(place, early, early_other, cols, rows, ph, pp, False)
    ph, pp = absorb(place, wrapped, late_other, cols, rows, ph, pp, False)
    return ph, pp


def solution(mesh):
    placed = (
        P("blk", None, None, None),
        P("blk", None),
        P("blk", None),
        P("blk", None),
        P(None, "blk", "grp", None),
        P(None, "blk", "grp", None),
    )
    return jax.shard_map(
        on_device,
        mesh=mesh,
        in_specs=placed,
        out_specs=(P(None, "blk", "grp", None), P(None, "blk", "grp", None)),
        check_vma=False,
    )
```

```python
import math

import jax
import jax.numpy as jnp
from jax import lax
from jax.experimental import pallas as pl
from jax.experimental.pallas import tpu as pltpu
from jax.sharding import PartitionSpec as P

NK = 16
ORDER = 256
BAND = 64
TRANS = 4
COUPLING = 0.5
BF = jnp.bfloat16
F32 = jnp.float32
MIB = 1 << 20
TINY = pl.CostEstimate(flops=1, bytes_accessed=1, transcendentals=0)


def wave(freq, mom, tau, site):
    turns = ((2 * freq + 1) * tau - 2 * mom * site) & 31
    phase = turns.astype(F32) * (math.pi / 16.0)
    return (jnp.cos(phase) * 0.0625).astype(BF), (jnp.sin(phase) * 0.0625).astype(BF)


def table_kernel(place_ref, shift_ref, flip_ref, cols_ref, rows_ref):
    square = (ORDER, ORDER)
    sub = lax.broadcasted_iota(jnp.int32, square, 0)
    lane = lax.broadcasted_iota(jnp.int32, square, 1)
    re, im = wave(lane >> 4, lane & 15, sub >> 4, sub & 15)
    cols_ref[2 * TRANS, :ORDER] = re
    cols_ref[2 * TRANS, ORDER:] = im
    re, im = wave(sub >> 4, sub & 15, lane >> 4, lane & 15)
    base = jnp.concatenate([re, im], 1)
    band_row = lax.broadcasted_iota(jnp.int32, (BAND, ORDER), 0) + place_ref[0] * BAND
    band_lane = lax.broadcasted_iota(jnp.int32, (BAND, ORDER), 1)

    def put_rows(slot, target):
        pick = jnp.where(band_lane == target, 1.0, 0.0).astype(BF)
        out = jnp.dot(pick, base, preferred_element_type=F32).astype(BF)
        rows_ref[2 * BAND * slot : 2 * BAND * slot + BAND] = out[:, :ORDER]
        rows_ref[2 * BAND * slot + BAND : 2 * BAND * (slot + 1)] = out[:, ORDER:]

    def put_cols(slot, target):
        pick = jnp.where(sub == target, 1.0, 0.0).astype(BF)
        cols_ref[slot] = jnp.dot(cols_ref[2 * TRANS], pick, preferred_element_type=F32).astype(BF)

    put_rows(0, band_row)
    for t in range(TRANS):
        freq, mom = shift_ref[t, 0] >> 4, shift_ref[t, 0] & 15

        def moved(i, freq=freq, mom=mom):
            return ((((i >> 4) + freq) & 15) << 4) + (((i & 15) + mom) & 15)

        put_rows(1 + t, moved(band_row))
        put_cols(t, moved(lane))
        freq, mom = flip_ref[t, 0] >> 4, flip_ref[t, 0] & 15

        def turned(i, freq=freq, mom=mom):
            return (((freq - (i >> 4)) & 15) << 4) + ((mom - (i & 15)) & 15)

        put_rows(1 + TRANS + t, turned(band_row))
        put_cols(TRANS + t, turned(lane))


def tables(place, shift, flip):
    return pl.pallas_call(
        table_kernel,
        out_shape=(
            jax.ShapeDtypeStruct((2 * TRANS + 1, 2 * ORDER, ORDER), BF),
            jax.ShapeDtypeStruct(((2 * TRANS + 1) * 2 * BAND, ORDER), BF),
        ),
        in_specs=[pl.BlockSpec(memory_space=pltpu.SMEM)] * 3,
        out_specs=(pl.BlockSpec(memory_space=pltpu.VMEM),) * 2,
        cost_estimate=TINY,
        compiler_params=pltpu.CompilerParams(vmem_limit_bytes=20 * MIB),
        name="tables",
    )(place, shift, flip)


def paired(re, im):
    return jnp.concatenate(
        [jnp.concatenate([re, im], 1), jnp.concatenate([im, -re], 1)], 0
    )


def halves(ref, begin):
    return paired(ref[begin : begin + BAND], ref[begin + BAND : begin + 2 * BAND])


def one_walker(up, down, cols, rows, ph, pp, first_up, first_down, plain):
    step = 2 * BAND
    first_up[...] = jnp.dot(rows[: step * (TRANS + 1)], up, preferred_element_type=F32).astype(BF)
    first_down[...] = jnp.dot(rows[step:], down, preferred_element_type=F32).astype(BF)
    across = (((1,), (1,)), ((), ()))
    turned_up = lax.dot_general(rows[:step], up, across, preferred_element_type=F32).astype(BF)
    turned_down = lax.dot_general(rows[:step], down, across, preferred_element_type=F32).astype(BF)
    left = jnp.concatenate(
        [halves(turned_up, 0), halves(turned_down, 0), halves(first_up, 0)], 0
    )
    plain[...] = jnp.dot(left, cols[2 * TRANS], preferred_element_type=F32)
    for t in range(TRANS):
        left = jnp.concatenate([halves(first_up, step * (1 + t)), halves(first_down, step * t)], 0)
        moved = jnp.dot(left, cols[t], preferred_element_type=F32)
        real, imag = 0.0, 0.0
        for s in range(2):
            nr, ni = plain[step * s : step * s + BAND], plain[step * s + BAND : step * (s + 1)]
            mr, mi = moved[step * s : step * s + BAND], moved[step * s + BAND : step * (s + 1)]
            real = real + (nr * mr + ni * mi)
            imag = imag + (nr * mi - ni * mr)
        ph[0, t] += real
        ph[1, t] += imag
        low = jnp.dot(
            halves(first_down, step * (TRANS + t)), cols[TRANS + t], preferred_element_type=F32
        )
        nr, ni = plain[2 * step : 2 * step + BAND], plain[2 * step + BAND : 3 * step]
        pp[0, t] += nr * low[:BAND] - ni * low[BAND:]
        pp[1, t] += nr * low[BAND:] + ni * low[:BAND]


def absorb_kernel(pieces, cols, rows, ph_in, pp_in, ph, pp, first_up, first_down, plain):
    ph[...] = ph_in[...]
    pp[...] = pp_in[...]
    for i in range(pieces.shape[0]):
        one_walker(pieces[i, 0], pieces[i, 1], cols, rows, ph, pp, first_up, first_down, plain)


def absorb(pieces, cols, rows, ph, pp, fresh):
    return pl.pallas_call(
        absorb_kernel,
        out_shape=(jax.ShapeDtypeStruct(ph.shape, F32), jax.ShapeDtypeStruct(pp.shape, F32)),
        in_specs=[pl.BlockSpec(memory_space=pltpu.VMEM)] * 5,
        out_specs=(pl.BlockSpec(memory_space=pltpu.VMEM),) * 2,
        scratch_shapes=[
            pltpu.VMEM((2 * BAND * (TRANS + 1), ORDER), BF),
            pltpu.VMEM((2 * BAND * 2 * TRANS, ORDER), BF),
            pltpu.VMEM((6 * BAND, ORDER), F32),
        ],
        input_output_aliases={} if fresh else {3: 0, 4: 1},
        cost_estimate=TINY,
        compiler_params=pltpu.CompilerParams(vmem_limit_bytes=24 * MIB),
        name="absorb",
    )(pieces, cols, rows, ph, pp)


def scale_kernel(masses, spins, out):
    signed = (2 * spins[...] - 1).astype(F32)
    for spin, sign in enumerate((COUPLING, -COUPLING)):
        factor = jnp.exp(sign * signed)
        out[spin] = (masses[0, spin].astype(F32) * factor).astype(BF)


def scale(masses, spins):
    return pl.pallas_call(
        scale_kernel,
        out_shape=jax.ShapeDtypeStruct((2, ORDER, ORDER), BF),
        in_specs=[pl.BlockSpec(memory_space=pltpu.VMEM)] * 2,
        out_specs=pl.BlockSpec(memory_space=pltpu.VMEM),
        cost_estimate=TINY,
        name="scale",
    )(masses, spins)


def route_kernel(place, y_ref, own, got, token, *outs):
    core = place[0] & 1
    for step, out in zip(Y_STEPS, outs):
        keep = (core == 0) | (y_ref[0] + step >= 4)

        @pl.when(keep)
        def _():
            out[...] = got[...]

        @pl.when(jnp.logical_not(keep))
        def _():
            out[...] = own[...]


def route(place, y, own, got, token):
    return pl.pallas_call(
        route_kernel,
        out_shape=(jax.ShapeDtypeStruct(own.shape, BF),) * 3,
        in_specs=[pl.BlockSpec(memory_space=pltpu.SMEM)] * 2
        + [pl.BlockSpec(memory_space=pltpu.VMEM)] * 2
        + [pl.BlockSpec(memory_space=pl.ANY)],
        out_specs=(pl.BlockSpec(memory_space=pltpu.VMEM),) * 3,
        cost_estimate=TINY,
        name="route",
    )(place, y, own, got, token)


Y_STEPS = (2, 1, 3)
PLANE = 4
BLOCKS = 64


def planes_back(value):
    pairs = [
        (g * BLOCKS + b, g * BLOCKS + (b + PLANE * (1 + g % 2)) % BLOCKS)
        for g in range(4)
        for b in range(BLOCKS)
    ]
    return lax.ppermute(value, ("grp", "blk"), pairs)


def along_y(value, steps):
    return lax.ppermute(value, "blk", [(s, s // 4 * 4 + (s + steps) % 4) for s in range(BLOCKS)])


def both_cores(value):
    return lax.all_gather(value, "grp", axis=0, axis_index_groups=[[0, 1], [2, 3]])


def on_device(masses, spins, shift_table, flip_table, ph_in, pp_in):
    place = lax.axis_index("grp").reshape(1).astype(jnp.int32)
    y = (lax.axis_index("blk") % PLANE).reshape(1).astype(jnp.int32)
    own = scale(masses, spins)
    got = planes_back(own)
    cols, rows = tables(place, shift_table, flip_table)
    ph, pp = absorb(own[None], cols, rows, ph_in, pp_in, True)
    got, ph, pp = lax.optimization_barrier((got, ph, pp))
    sent = route(place, y, own, got, ph)
    across = [along_y(v, d) for v, d in zip(sent, Y_STEPS)]
    ph, pp = absorb(both_cores(got), cols, rows, ph, pp, False)
    for piece in across:
        piece, ph, pp = lax.optimization_barrier((piece, ph, pp))
        ph, pp = absorb(both_cores(piece), cols, rows, ph, pp, False)
    return ph, pp


def solution(mesh):
    placed = (
        P("blk", None, None, None),
        P("blk", None),
        P("blk", None),
        P("blk", None),
        P(None, "blk", "grp", None),
        P(None, "blk", "grp", None),
    )
    return jax.shard_map(
        on_device,
        mesh=mesh,
        in_specs=placed,
        out_specs=(P(None, "blk", "grp", None), P(None, "blk", "grp", None)),
        check_vma=False,
    )
```

```python
import functools
import math

import jax
import jax.numpy as jnp
from jax import lax
from jax.experimental import pallas as pl
from jax.experimental.pallas import tpu as pltpu
from jax.sharding import PartitionSpec as P

NK = 16
ORDER = 256
BAND = 64
TRANS = 4
COUPLING = 0.5
BF = jnp.bfloat16
F32 = jnp.float32
MIB = 1 << 20
TINY = pl.CostEstimate(flops=1, bytes_accessed=1, transcendentals=0)


def wave(freq, mom, tau, site):
    turns = ((2 * freq + 1) * tau - 2 * mom * site) & 31
    phase = turns.astype(F32) * (math.pi / 16.0)
    return (jnp.cos(phase) * 0.0625).astype(BF), (jnp.sin(phase) * 0.0625).astype(BF)


def table_kernel(place_ref, shift_in, flip_in, cols_ref, rows_ref, shift_ref, flip_ref, sems):
    fetch = [
        pltpu.make_async_copy(shift_in, shift_ref, sems.at[0]),
        pltpu.make_async_copy(flip_in, flip_ref, sems.at[1]),
    ]
    for copy in fetch:
        copy.start()
    square = (ORDER, ORDER)
    sub = lax.broadcasted_iota(jnp.int32, square, 0)
    lane = lax.broadcasted_iota(jnp.int32, square, 1)
    re, im = wave(lane >> 4, lane & 15, sub >> 4, sub & 15)
    cols_ref[2 * TRANS, :ORDER] = re
    cols_ref[2 * TRANS, ORDER:] = im
    re, im = wave(sub >> 4, sub & 15, lane >> 4, lane & 15)
    base = jnp.concatenate([re, im], 1)
    band_row = lax.broadcasted_iota(jnp.int32, (BAND, ORDER), 0) + place_ref[0] * BAND
    band_lane = lax.broadcasted_iota(jnp.int32, (BAND, ORDER), 1)

    def put_rows(slot, target):
        pick = jnp.where(band_lane == target, 1.0, 0.0).astype(BF)
        out = jnp.dot(pick, base, preferred_element_type=F32).astype(BF)
        rows_ref[2 * BAND * slot : 2 * BAND * slot + BAND] = out[:, :ORDER]
        rows_ref[2 * BAND * slot + BAND : 2 * BAND * (slot + 1)] = out[:, ORDER:]

    def put_cols(slot, target):
        pick = jnp.where(sub == target, 1.0, 0.0).astype(BF)
        cols_ref[slot] = jnp.dot(cols_ref[2 * TRANS], pick, preferred_element_type=F32).astype(BF)

    put_rows(0, band_row)
    for copy in fetch:
        copy.wait()
    for t in range(TRANS):
        freq, mom = shift_ref[t, 0] >> 4, shift_ref[t, 0] & 15

        def moved(i, freq=freq, mom=mom):
            return ((((i >> 4) + freq) & 15) << 4) + (((i & 15) + mom) & 15)

        put_rows(1 + t, moved(band_row))
        put_cols(t, moved(lane))
        freq, mom = flip_ref[t, 0] >> 4, flip_ref[t, 0] & 15

        def turned(i, freq=freq, mom=mom):
            return (((freq - (i >> 4)) & 15) << 4) + ((mom - (i & 15)) & 15)

        put_rows(1 + TRANS + t, turned(band_row))
        put_cols(TRANS + t, turned(lane))


def tables(place, shift, flip):
    return pl.pallas_call(
        table_kernel,
        out_shape=(
            jax.ShapeDtypeStruct((2 * TRANS + 1, 2 * ORDER, ORDER), BF),
            jax.ShapeDtypeStruct(((2 * TRANS + 1) * 2 * BAND, ORDER), BF),
        ),
        in_specs=[
            pl.BlockSpec(memory_space=pltpu.SMEM),
            pl.BlockSpec(memory_space=pltpu.HBM),
            pl.BlockSpec(memory_space=pltpu.HBM),
        ],
        out_specs=(pl.BlockSpec(memory_space=pltpu.VMEM),) * 2,
        scratch_shapes=[
            pltpu.SMEM((TRANS, ORDER), jnp.int32),
            pltpu.SMEM((TRANS, ORDER), jnp.int32),
            pltpu.SemaphoreType.DMA((2,)),
        ],
        cost_estimate=pl.CostEstimate(flops=4 * 10**9, bytes_accessed=1, transcendentals=0),
        compiler_params=pltpu.CompilerParams(vmem_limit_bytes=12 * MIB),
        name="tables",
    )(place, shift, flip)


def paired(re, im):
    return jnp.concatenate(
        [jnp.concatenate([re, im], 1), jnp.concatenate([im, -re], 1)], 0
    )


def halves(ref, begin):
    return paired(ref[begin : begin + BAND], ref[begin + BAND : begin + 2 * BAND])


def one_walker(up, down, cols, rows, first_up, first_down, plain, ready, put):
    step = 2 * BAND
    first_up[...] = jnp.dot(rows[: step * (TRANS + 1)], up, preferred_element_type=F32).astype(BF)
    first_down[...] = jnp.dot(rows[step:], down, preferred_element_type=F32).astype(BF)
    across = (((1,), (1,)), ((), ()))
    turned_up = lax.dot_general(rows[:step], up, across, preferred_element_type=F32).astype(BF)
    turned_down = lax.dot_general(rows[:step], down, across, preferred_element_type=F32).astype(BF)
    left = jnp.concatenate(
        [halves(turned_up, 0), halves(turned_down, 0), halves(first_up, 0)], 0
    )
    plain[...] = jnp.dot(left, cols[2 * TRANS], preferred_element_type=F32)
    ready()
    for t in range(TRANS):
        left = jnp.concatenate([halves(first_up, step * (1 + t)), halves(first_down, step * t)], 0)
        moved = jnp.dot(left, cols[t], preferred_element_type=F32)
        real, imag = 0.0, 0.0
        for s in range(2):
            nr, ni = plain[step * s : step * s + BAND], plain[step * s + BAND : step * (s + 1)]
            mr, mi = moved[step * s : step * s + BAND], moved[step * s + BAND : step * (s + 1)]
            real = real + (nr * mr + ni * mi)
            imag = imag + (nr * mi - ni * mr)
        put(0, 0, t, real)
        put(0, 1, t, imag)
        low = jnp.dot(
            halves(first_down, step * (TRANS + t)), cols[TRANS + t], preferred_element_type=F32
        )
        nr, ni = plain[2 * step : 2 * step + BAND], plain[2 * step + BAND : 3 * step]
        put(1, 0, t, nr * low[:BAND] - ni * low[BAND:])
        put(1, 1, t, nr * low[BAND:] + ni * low[:BAND])


WORK = [
    pltpu.VMEM((2 * BAND * (TRANS + 1), ORDER), BF),
    pltpu.VMEM((2 * BAND * 2 * TRANS, ORDER), BF),
    pltpu.VMEM((6 * BAND, ORDER), F32),
]
SUMS = (2, TRANS, BAND, ORDER)
IN_VMEM = pl.BlockSpec(memory_space=pltpu.VMEM)
IN_SMEM = pl.BlockSpec(memory_space=pltpu.SMEM)
ANYWHERE = pl.BlockSpec(memory_space=pl.ANY)
IN_HBM = pl.BlockSpec(memory_space=pltpu.HBM)
BIG = pltpu.CompilerParams(vmem_limit_bytes=16 * MIB)


def open_kernel(
    piece, cols, rows, ph_in, pp_in, ph, pp, token, first_up, first_down, plain, sems
):
    loads = [
        pltpu.make_async_copy(source.at[part], target.at[part], sems.at[i, part])
        for i, (source, target) in enumerate(((ph_in, ph), (pp_in, pp)))
        for part in range(2)
    ]
    for load in loads:
        load.start()

    def ready():
        for load in loads:
            load.wait()

    def put(which, part, t, term):
        (ph, pp)[which][part, t] += term

    one_walker(piece[0], piece[1], cols, rows, first_up, first_down, plain, ready, put)
    token[...] = jnp.zeros_like(token)


def open_sums(piece, cols, rows, ph, pp):
    return pl.pallas_call(
        open_kernel,
        out_shape=(jax.ShapeDtypeStruct(SUMS, F32),) * 2
        + (jax.ShapeDtypeStruct((8, 128), F32),),
        in_specs=[IN_VMEM] * 3 + [IN_HBM] * 2,
        out_specs=(IN_VMEM,) * 3,
        scratch_shapes=WORK + [pltpu.SemaphoreType.DMA((2, 2))],
        cost_estimate=TINY,
        compiler_params=BIG,
        name="open_sums",
    )(piece, cols, rows, ph, pp)


def add_kernel(names, held, place, *refs):
    count = len(names["in"])
    pieces, (cols, rows, ph_in, pp_in, ph, pp) = refs[:count], refs[count : count + 6]
    kept, (first_up, first_down, plain) = refs[count + 6 : -3], refs[-3:]
    other = 1 - (place[0] & 1)
    for i, sheet in enumerate(held):
        piece, spin = sheet
        kept[i // 3][i % 3] = pieces[piece][spin]
    first = True
    for walker in names["walkers"]:
        if names["gathered"]:
            up, down = [pieces[w // 3][other, w % 3] for w in (2 * walker, 2 * walker + 1)]
        else:
            up, down = pieces[walker][0], pieces[walker][1]

        def put(which, part, t, term, first=first):
            source = (ph_in, pp_in) if first else (ph, pp)
            (ph, pp)[which][part, t] = source[which][part, t] + term

        one_walker(up, down, cols, rows, first_up, first_down, plain, lambda: None, put)
        first = False


def add(place, pieces, cols, rows, ph, pp, walkers, held=(), gathered=False):
    count = len(pieces)
    out_shape = [jax.ShapeDtypeStruct(SUMS, F32)] * 2
    out_shape += [jax.ShapeDtypeStruct((3, ORDER, ORDER), BF)] * (len(held) // 3)
    names = {"in": range(count), "walkers": walkers, "gathered": gathered}
    return pl.pallas_call(
        functools.partial(add_kernel, names, held),
        out_shape=tuple(out_shape),
        in_specs=[IN_SMEM] + [IN_VMEM] * (count + 4),
        out_specs=(IN_VMEM,) * len(out_shape),
        scratch_shapes=WORK,
        cost_estimate=TINY,
        compiler_params=BIG,
        name="add",
    )(place, *pieces, cols, rows, ph, pp)


def close_kernel(
    piece, cols, rows, ph_in, pp_in, ph, pp, first_up, first_down, plain, ph_sum, pp_sum, sems
):
    stores = []

    def put(which, part, t, term):
        source, total, target = ((ph_in, ph_sum, ph), (pp_in, pp_sum, pp))[which]
        total[part, t] = source[part, t] + term
        store = pltpu.make_async_copy(
            total.at[part, t], target.at[part, t], sems.at[which, part, t]
        )
        store.start()
        stores.append(store)

    one_walker(piece[0], piece[1], cols, rows, first_up, first_down, plain, lambda: None, put)
    for store in stores:
        store.wait()


def close_sums(piece, cols, rows, ph, pp):
    return pl.pallas_call(
        close_kernel,
        out_shape=(jax.ShapeDtypeStruct(SUMS, F32),) * 2,
        in_specs=[IN_VMEM] * 5,
        out_specs=(ANYWHERE,) * 2,
        scratch_shapes=WORK
        + [pltpu.VMEM(SUMS, F32)] * 2
        + [pltpu.SemaphoreType.DMA((2, 2, TRANS))],
        cost_estimate=TINY,
        compiler_params=BIG,
        name="close_sums",
    )(piece, cols, rows, ph, pp)


def scale_kernel(masses, spins, out):
    signed = (2 * spins[...] - 1).astype(F32)
    sign = jnp.where(pl.program_id(0) < 2, COUPLING, -COUPLING)
    out[0] = (masses[0, 0].astype(F32) * jnp.exp(sign * signed)).astype(BF)


def scale(masses, spins):
    half = ORDER // 2
    return pl.pallas_call(
        scale_kernel,
        grid=(4,),
        out_shape=jax.ShapeDtypeStruct((2, ORDER, ORDER), BF),
        in_specs=[
            pl.BlockSpec((1, 1, half, ORDER), lambda i: (0, i // 2, i % 2, 0)),
            pl.BlockSpec((1, ORDER), lambda i: (0, 0)),
        ],
        out_specs=pl.BlockSpec((1, half, ORDER), lambda i: (i // 2, i % 2, 0)),
        cost_estimate=TINY,
        compiler_params=pltpu.CompilerParams(vmem_limit_bytes=56 * MIB),
        name="scale",
    )(masses, spins)


def route_kernel(place, y_ref, own, got, token, *refs):
    outs, sems = refs[:3], refs[3]
    core = place[0] & 1
    for i, step in enumerate(Y_STEPS):
        keep = (core == 0) | (y_ref[0] + step >= PLANE)

        @pl.when(keep)
        def _(i=i):
            pltpu.make_async_copy(got, outs[i], sems.at[i]).start()

        @pl.when(jnp.logical_not(keep))
        def _(i=i):
            pltpu.make_async_copy(own, outs[i], sems.at[i]).start()

    for i in range(3):
        pltpu.make_async_copy(own, outs[i], sems.at[i]).wait()


def route(place, y, own, got, token):
    return pl.pallas_call(
        route_kernel,
        out_shape=(jax.ShapeDtypeStruct(own.shape, BF),) * 3,
        in_specs=[IN_SMEM] * 2 + [ANYWHERE] * 3,
        out_specs=(ANYWHERE,) * 3,
        scratch_shapes=[pltpu.SemaphoreType.DMA((3,))],
        cost_estimate=TINY,
        compiler_params=pltpu.CompilerParams(vmem_limit_bytes=MIB),
        name="route",
    )(place, y, own, got, token)


Y_STEPS = (1, 3, 2)
PLANE = 4
BLOCKS = 64


def planes_back(value):
    pairs = [
        (g * BLOCKS + b, g * BLOCKS + (b + PLANE * (1 + g % 2)) % BLOCKS)
        for g in range(4)
        for b in range(BLOCKS)
    ]
    return lax.ppermute(value, ("grp", "blk"), pairs)


def along_y(value, steps):
    return lax.ppermute(value, "blk", [(s, s // 4 * 4 + (s + steps) % 4) for s in range(BLOCKS)])


def both_cores(value):
    return lax.all_gather(value, "grp", axis=0, axis_index_groups=[[0, 1], [2, 3]])


def other_core(value):
    return lax.ppermute(value, "grp", [(s, s ^ 1) for s in range(4)])


def on_device(masses, spins, shift_table, flip_table, ph_in, pp_in):
    place = lax.axis_index("grp").reshape(1).astype(jnp.int32)
    y = (lax.axis_index("blk") % PLANE).reshape(1).astype(jnp.int32)
    own = scale(masses, spins)
    got = planes_back(own)
    cols, rows = tables(place, shift_table, flip_table)
    ph, pp, token = open_sums(own, cols, rows, ph_in, pp_in)
    got, token = lax.optimization_barrier((got, token))
    sent = route(place, y, own, got, token)
    right, left, middle = [along_y(v, d) for v, d in zip(sent, Y_STEPS)]
    ph, pp = add(place, [got], cols, rows, ph, pp, (0,))
    right, left, ph, pp = lax.optimization_barrier((right, left, ph, pp))
    sheets = tuple((piece, spin) for piece in range(3) for spin in range(2))
    ph, pp, *held = add(place, [got, right, left], cols, rows, ph, pp, (1, 2), sheets)
    held = [both_cores(v) for v in held]
    ph, pp = add(place, held, cols, rows, ph, pp, (0, 1, 2), gathered=True)
    middle, ph, pp = lax.optimization_barrier((middle, ph, pp))
    swapped = other_core(middle)
    ph, pp = add(place, [middle], cols, rows, ph, pp, (0,))
    return close_sums(swapped, cols, rows, ph, pp)


def solution(mesh):
    placed = (
        P("blk", None, None, None),
        P("blk", None),
        P("blk", None),
        P("blk", None),
        P(None, "blk", "grp", None),
        P(None, "blk", "grp", None),
    )
    return jax.shard_map(
        on_device,
        mesh=mesh,
        in_specs=placed,
        out_specs=(P(None, "blk", "grp", None), P(None, "blk", "grp", None)),
        check_vma=False,
    )
```

```python
import functools
import math

import jax
import jax.numpy as jnp
from jax import lax
from jax.experimental import pallas as pl
from jax.experimental.pallas import tpu as pltpu
from jax.sharding import PartitionSpec as P

NK = 16
ORDER = 256
BAND = 64
TRANS = 4
COUPLING = 0.5
BF = jnp.bfloat16
F32 = jnp.float32
MIB = 1 << 20
TINY = pl.CostEstimate(flops=1, bytes_accessed=1, transcendentals=0)


def wave(freq, mom, tau, site):
    turns = ((2 * freq + 1) * tau - 2 * mom * site) & 31
    phase = turns.astype(F32) * (math.pi / 16.0)
    return (jnp.cos(phase) * 0.0625).astype(BF), (jnp.sin(phase) * 0.0625).astype(BF)


def table_kernel(
    place_ref, shift_in, flip_in, cols_ref, rows_ref, shift_ref, flip_ref, sems
):
    fetch = [
        pltpu.make_async_copy(shift_in, shift_ref, sems.at[0]),
        pltpu.make_async_copy(flip_in, flip_ref, sems.at[1]),
    ]
    for copy in fetch:
        copy.start()
    square = (ORDER, ORDER)
    sub = lax.broadcasted_iota(jnp.int32, square, 0)
    lane = lax.broadcasted_iota(jnp.int32, square, 1)
    re, im = wave(lane >> 4, lane & 15, sub >> 4, sub & 15)
    cols_ref[2 * TRANS, :ORDER] = re
    cols_ref[2 * TRANS, ORDER:] = im
    re, im = wave(sub >> 4, sub & 15, lane >> 4, lane & 15)
    base = jnp.concatenate([re, im], 1)
    both = lax.broadcasted_iota(jnp.int32, (2 * BAND, ORDER), 0)
    grp = jnp.where(both < BAND, place_ref[0], place_ref[0] ^ 1)
    band_row = (both & (BAND - 1)) + grp * BAND
    band_lane = lax.broadcasted_iota(jnp.int32, (2 * BAND, ORDER), 1)

    def put_rows(slot, target):
        pick = jnp.where(band_lane == target, 1.0, 0.0).astype(BF)
        out = jnp.dot(pick, base, preferred_element_type=F32).astype(BF)
        for b in range(2):
            part = out[BAND * b : BAND * (b + 1)]
            rows_ref[b, 2 * BAND * slot : 2 * BAND * slot + BAND] = part[:, :ORDER]
            rows_ref[b, 2 * BAND * slot + BAND : 2 * BAND * (slot + 1)] = part[:, ORDER:]

    def put_cols(slot, target):
        pick = jnp.where(sub == target, 1.0, 0.0).astype(BF)
        cols_ref[slot] = jnp.dot(cols_ref[2 * TRANS], pick, preferred_element_type=F32).astype(BF)

    put_rows(0, band_row)
    for copy in fetch:
        copy.wait()
    for t in range(TRANS):
        freq, mom = shift_ref[t, 0] >> 4, shift_ref[t, 0] & 15

        def moved(i, freq=freq, mom=mom):
            return ((((i >> 4) + freq) & 15) << 4) + (((i & 15) + mom) & 15)

        put_rows(1 + t, moved(band_row))
        put_cols(t, moved(lane))
        freq, mom = flip_ref[t, 0] >> 4, flip_ref[t, 0] & 15

        def turned(i, freq=freq, mom=mom):
            return (((freq - (i >> 4)) & 15) << 4) + ((mom - (i & 15)) & 15)

        put_rows(1 + TRANS + t, turned(band_row))
        put_cols(TRANS + t, turned(lane))


def tables(place, shift, flip):
    return pl.pallas_call(
        table_kernel,
        out_shape=(
            jax.ShapeDtypeStruct((2 * TRANS + 1, 2 * ORDER, ORDER), BF),
            jax.ShapeDtypeStruct((2, (2 * TRANS + 1) * 2 * BAND, ORDER), BF),
        ),
        in_specs=[
            pl.BlockSpec(memory_space=pltpu.SMEM),
            pl.BlockSpec(memory_space=pltpu.HBM),
            pl.BlockSpec(memory_space=pltpu.HBM),
        ],
        out_specs=(pl.BlockSpec(memory_space=pltpu.VMEM),) * 2,
        scratch_shapes=[
            pltpu.SMEM((TRANS, ORDER), jnp.int32),
            pltpu.SMEM((TRANS, ORDER), jnp.int32),
            pltpu.SemaphoreType.DMA((2,)),
        ],
        cost_estimate=pl.CostEstimate(flops=4 * 10**9, bytes_accessed=1, transcendentals=0),
        compiler_params=pltpu.CompilerParams(vmem_limit_bytes=12 * MIB),
        name="tables",
    )(place, shift, flip)


def paired(re, im):
    return jnp.concatenate(
        [jnp.concatenate([re, im], 1), jnp.concatenate([im, -re], 1)], 0
    )


def halves(ref, begin):
    return paired(ref[begin : begin + BAND], ref[begin + BAND : begin + 2 * BAND])


def one_walker(up, down, cols, rows, first_up, first_down, plain, ready, put):
    step = 2 * BAND
    first_up[...] = jnp.dot(rows[: step * (TRANS + 1)], up, preferred_element_type=F32).astype(BF)
    first_down[...] = jnp.dot(rows[step:], down, preferred_element_type=F32).astype(BF)
    across = (((1,), (1,)), ((), ()))
    turned_up = lax.dot_general(rows[:step], up, across, preferred_element_type=F32).astype(BF)
    turned_down = lax.dot_general(rows[:step], down, across, preferred_element_type=F32).astype(BF)
    left = jnp.concatenate(
        [halves(turned_up, 0), halves(turned_down, 0), halves(first_up, 0)], 0
    )
    plain[...] = jnp.dot(left, cols[2 * TRANS], preferred_element_type=F32)
    ready()
    for t in range(TRANS):
        left = jnp.concatenate([halves(first_up, step * (1 + t)), halves(first_down, step * t)], 0)
        moved = jnp.dot(left, cols[t], preferred_element_type=F32)
        real, imag = 0.0, 0.0
        for s in range(2):
            nr, ni = plain[step * s : step * s + BAND], plain[step * s + BAND : step * (s + 1)]
            mr, mi = moved[step * s : step * s + BAND], moved[step * s + BAND : step * (s + 1)]
            real = real + (nr * mr + ni * mi)
            imag = imag + (nr * mi - ni * mr)
        put(0, 0, t, real)
        put(0, 1, t, imag)
        low = jnp.dot(
            halves(first_down, step * (TRANS + t)), cols[TRANS + t], preferred_element_type=F32
        )
        nr, ni = plain[2 * step : 2 * step + BAND], plain[2 * step + BAND : 3 * step]
        put(1, 0, t, nr * low[:BAND] - ni * low[BAND:])
        put(1, 1, t, nr * low[BAND:] + ni * low[:BAND])


WORK = [
    pltpu.VMEM((2 * BAND * (TRANS + 1), ORDER), BF),
    pltpu.VMEM((2 * BAND * 2 * TRANS, ORDER), BF),
    pltpu.VMEM((6 * BAND, ORDER), F32),
]
SUMS = (2, TRANS, BAND, ORDER)
PIECE = (2, ORDER, ORDER)
IN_VMEM = pl.BlockSpec(memory_space=pltpu.VMEM)
IN_SMEM = pl.BlockSpec(memory_space=pltpu.SMEM)
ANYWHERE = pl.BlockSpec(memory_space=pl.ANY)
IN_HBM = pl.BlockSpec(memory_space=pltpu.HBM)
BIG = pltpu.CompilerParams(vmem_limit_bytes=16 * MIB)


def open_kernel(piece, cols, rows, ph_in, pp_in, sums, first_up, first_down, plain, sems):
    loads = [
        pltpu.make_async_copy(source.at[part], sums.at[i, part], sems.at[i, part])
        for i, source in enumerate((ph_in, pp_in))
        for part in range(2)
    ]
    for load in loads:
        load.start()

    def ready():
        for load in loads:
            load.wait()

    def put(which, part, t, term):
        sums[which, part, t] += term

    one_walker(piece[0], piece[1], cols, rows.at[0], first_up, first_down, plain, ready, put)


def open_sums(piece, cols, rows, ph, pp):
    return pl.pallas_call(
        open_kernel,
        out_shape=jax.ShapeDtypeStruct((2, *SUMS), F32),
        in_specs=[IN_VMEM] * 3 + [IN_HBM] * 2,
        out_specs=IN_VMEM,
        scratch_shapes=WORK + [pltpu.SemaphoreType.DMA((2, 2))],
        cost_estimate=TINY,
        compiler_params=BIG,
        name="open_sums",
    )(piece, cols, rows, ph, pp)


def fetch_lane(core, pair, hold, sem):
    for c in range(2):

        @pl.when(core == c)
        def _(c=c):
            pltpu.make_async_copy(pair[c], hold, sem).start()


def spread_kernel(count, fresh, send, place, *refs):
    pairs = [refs[2 * i : 2 * i + 2] for i in range(count)]
    cols, rows, before = refs[2 * count : 2 * count + 3]
    after = refs[2 * count + 3 : 2 * count + 4 + send]
    first_up, first_down, plain, hold, sems, *held = refs[2 * count + 4 + send :]
    core = place[0] & 1
    for n, pair in enumerate(pairs):
        fetch_lane(core, pair, hold.at[n], sems.at[n])
    for n, pair in enumerate(pairs):
        pltpu.make_async_copy(pair[0], hold.at[n], sems.at[n]).wait()
        for b in range(2):

            def put(which, part, t, term, n=n, b=b):
                if n == 0:
                    if not (fresh and b):
                        term = term + before[2 * b + which, part, t]
                elif send and b:
                    term = term + held[0][which, part, t]
                else:
                    term = term + after[0][2 * b + which, part, t]
                if not (send and b):
                    after[0][2 * b + which, part, t] = term
                elif n < count - 1:
                    held[0][which, part, t] = term
                else:
                    after[1][which, part, t] = term.astype(BF)

            one_walker(
                hold[n, 0], hold[n, 1], cols, rows.at[b], first_up, first_down, plain,
                lambda: None, put,
            )


def spread(place, pairs, cols, rows, sums, send=False):
    count, fresh = len(pairs), sums.shape[0] == 2
    out_shape = [jax.ShapeDtypeStruct((2 if send else 4, *SUMS), F32)]
    if send:
        out_shape.append(jax.ShapeDtypeStruct((2, *SUMS), BF))
    return pl.pallas_call(
        functools.partial(spread_kernel, count, fresh, send),
        out_shape=tuple(out_shape),
        in_specs=[IN_SMEM] + [ANYWHERE] * (2 * count) + [IN_VMEM] * 3,
        out_specs=(IN_VMEM,) * len(out_shape),
        scratch_shapes=WORK
        + [pltpu.VMEM((count, *PIECE), BF), pltpu.SemaphoreType.DMA((count,))]
        + [pltpu.VMEM((2, *SUMS), F32)] * send,
        cost_estimate=TINY,
        compiler_params=BIG,
        name="spread",
    )(place, *[piece for pair in pairs for piece in pair], cols, rows, sums)


def add_kernel(place, lane0, lane1, cols, rows, before, after, first_up, first_down, plain, hold, sem):
    fetch_lane(place[0] & 1, (lane0, lane1), hold, sem.at[0])
    pltpu.make_async_copy(lane0, hold, sem.at[0]).wait()

    def put(which, part, t, term):
        after[which, part, t] = before[which, part, t] + term

    one_walker(
        hold[0], hold[1], cols, rows.at[0], first_up, first_down, plain, lambda: None, put
    )


def add(place, pair, cols, rows, sums):
    return pl.pallas_call(
        add_kernel,
        out_shape=jax.ShapeDtypeStruct((2, *SUMS), F32),
        in_specs=[IN_SMEM] + [ANYWHERE] * 2 + [IN_VMEM] * 3,
        out_specs=IN_VMEM,
        scratch_shapes=WORK + [pltpu.VMEM(PIECE, BF), pltpu.SemaphoreType.DMA((1,))],
        cost_estimate=TINY,
        compiler_params=BIG,
        name="add",
    )(place, *pair, cols, rows, sums)


def close_kernel(
    place, lane0, lane1, cols, rows, sums, others, ph, pp,
    first_up, first_down, plain, hold, sem, total, sems,
):
    fetch_lane(place[0] & 1, (lane0, lane1), hold, sem.at[0])
    pltpu.make_async_copy(lane0, hold, sem.at[0]).wait()
    stores = []

    def put(which, part, t, term):
        other = others[which, part, t].astype(F32)
        total[which, part, t] = sums[which, part, t] + other + term
        store = pltpu.make_async_copy(
            total.at[which, part, t], (ph, pp)[which].at[part, t], sems.at[which, part, t]
        )
        store.start()
        stores.append(store)

    one_walker(
        hold[0], hold[1], cols, rows.at[0], first_up, first_down, plain, lambda: None, put
    )
    for store in stores:
        store.wait()


def close_sums(place, pair, cols, rows, sums, others):
    return pl.pallas_call(
        close_kernel,
        out_shape=(jax.ShapeDtypeStruct(SUMS, F32),) * 2,
        in_specs=[IN_SMEM] + [ANYWHERE] * 2 + [IN_VMEM] * 4,
        out_specs=(ANYWHERE,) * 2,
        scratch_shapes=WORK
        + [pltpu.VMEM(PIECE, BF), pltpu.SemaphoreType.DMA((1,))]
        + [pltpu.VMEM((2, *SUMS), F32), pltpu.SemaphoreType.DMA((2, 2, TRANS))],
        cost_estimate=TINY,
        compiler_params=BIG,
        name="close_sums",
    )(place, *pair, cols, rows, sums, others)


def scale_kernel(masses, spins, out, raw, done, in_sems, out_sems):
    half = ORDER // 2
    parts = [(spin, pl.ds(begin, half)) for spin in range(2) for begin in (0, half)]
    loads = [
        pltpu.make_async_copy(masses.at[0, spin, rows], raw.at[spin, rows], in_sems.at[i])
        for i, (spin, rows) in enumerate(parts)
    ]
    stores = [
        pltpu.make_async_copy(done.at[spin, rows], out.at[spin, rows], out_sems.at[i])
        for i, (spin, rows) in enumerate(parts)
    ]
    for load in loads:
        load.start()
    signed = (2 * spins[...] - 1).astype(F32)
    factors = jnp.exp(COUPLING * signed), jnp.exp(-COUPLING * signed)
    for (spin, rows), load, store in zip(parts, loads, stores):
        load.wait()
        done[spin, rows] = (raw[spin, rows].astype(F32) * factors[spin]).astype(BF)
        store.start()
    for store in stores:
        store.wait()


def scale(masses, spins):
    return pl.pallas_call(
        scale_kernel,
        out_shape=jax.ShapeDtypeStruct((2, ORDER, ORDER), BF),
        in_specs=[ANYWHERE, IN_VMEM],
        out_specs=ANYWHERE,
        scratch_shapes=[pltpu.VMEM((2, ORDER, ORDER), BF)] * 2
        + [pltpu.SemaphoreType.DMA((4,))] * 2,
        cost_estimate=TINY,
        compiler_params=pltpu.CompilerParams(vmem_limit_bytes=56 * MIB),
        name="scale",
    )(masses, spins)


def route_kernel(steps, y_ref, own, got, after, *refs):
    outs, sems = refs[: len(steps)], refs[len(steps)]
    for i, step in enumerate(steps):
        wraps = y_ref[0] + step >= PLANE

        @pl.when(wraps)
        def _(i=i):
            pltpu.make_async_copy(got, outs[i], sems.at[i]).start()

        @pl.when(jnp.logical_not(wraps))
        def _(i=i):
            pltpu.make_async_copy(own, outs[i], sems.at[i]).start()

    for i in range(len(steps)):
        pltpu.make_async_copy(own, outs[i], sems.at[i]).wait()


def route(y, own, got, after, steps):
    return pl.pallas_call(
        functools.partial(route_kernel, steps),
        out_shape=(jax.ShapeDtypeStruct(own.shape, BF),) * len(steps),
        in_specs=[IN_SMEM] + [ANYWHERE] * 2 + [IN_VMEM],
        out_specs=(ANYWHERE,) * len(steps),
        scratch_shapes=[pltpu.SemaphoreType.DMA((len(steps),))],
        cost_estimate=TINY,
        compiler_params=pltpu.CompilerParams(vmem_limit_bytes=MIB),
        name="route",
    )(y, own, got, after)


PLANE = 4
BLOCKS = 64


def move(value, pairs):
    flat = [(a * BLOCKS + b, c * BLOCKS + d) for (a, b), (c, d) in pairs]
    return lax.ppermute(value, ("grp", "blk"), flat)


def next_plane(value, core):
    return move(
        value,
        [((g, b), (g + core, (b + PLANE) % BLOCKS)) for g in (0, 2) for b in range(BLOCKS)],
    )


def along_y(value, steps, core):
    return move(
        value,
        [
            ((g + core, b), (g + core, b // PLANE * PLANE + (b + steps) % PLANE))
            for g in (0, 2)
            for b in range(BLOCKS)
        ],
    )


def other_core(value, cores=(0, 1)):
    return lax.ppermute(value, "grp", [(s, s ^ 1) for s in range(4) if s % 2 in cores])


def on_device(masses, spins, shift_table, flip_table, ph_in, pp_in):
    place = lax.axis_index("grp").reshape(1).astype(jnp.int32)
    y = (lax.axis_index("blk") % PLANE).reshape(1).astype(jnp.int32)
    own = scale(masses, spins)
    near = next_plane(own, 0)
    cols, rows = tables(place, shift_table, flip_table)
    near, cols = lax.optimization_barrier((near, cols))
    far = next_plane(near, 1)
    right0, left0 = along_y(near, 1, 0), along_y(near, 3, 0)
    sums = open_sums(own, cols, rows, ph_in, pp_in)
    far, sums = lax.optimization_barrier((far, sums))
    right, left, middle = route(y, own, far, sums, (1, 3, 2))
    middle0 = along_y(near, 2, 0)
    right1, left1 = along_y(right, 1, 1), along_y(left, 3, 1)
    (sums,) = spread(place, [(near, far)], cols, rows, sums)
    middle, sums = lax.optimization_barrier((middle, sums))
    middle1 = along_y(middle, 2, 1)
    right0, left0, right1, left1, sums = lax.optimization_barrier(
        (right0, left0, right1, left1, sums)
    )
    sums, sent = spread(place, [(right0, right1), (left0, left1)], cols, rows, sums, True)
    others = other_core(sent)
    middle0, middle1, sums = lax.optimization_barrier((middle0, middle1, sums))
    swapped = other_core(middle1, (1,)), other_core(middle0, (0,))
    sums = add(place, (middle0, middle1), cols, rows, sums)
    return close_sums(place, swapped, cols, rows, sums, others)


def solution(mesh):
    placed = (
        P("blk", None, None, None),
        P("blk", None),
        P("blk", None),
        P("blk", None),
        P(None, "blk", "grp", None),
        P(None, "blk", "grp", None),
    )
    return jax.shard_map(
        on_device,
        mesh=mesh,
        in_specs=placed,
        out_specs=(P(None, "blk", "grp", None), P(None, "blk", "grp", None)),
        check_vma=False,
    )
```

```python
import functools
import math

import jax
import jax.numpy as jnp
from jax import lax
from jax.experimental import pallas as pl
from jax.experimental.pallas import tpu as pltpu
from jax.sharding import PartitionSpec as P

NK = 16
ORDER = 256
BAND = 64
TRANS = 4
COUPLING = 0.5
BF = jnp.bfloat16
F32 = jnp.float32
MIB = 1 << 20
TINY = pl.CostEstimate(flops=1, bytes_accessed=1, transcendentals=0)


def wave(freq, mom, tau, site):
    turns = ((2 * freq + 1) * tau - 2 * mom * site) & 31
    phase = turns.astype(F32) * (math.pi / 16.0)
    return (jnp.cos(phase) * 0.0625).astype(BF), (jnp.sin(phase) * 0.0625).astype(BF)


def table_kernel(
    place_ref, shift_in, flip_in, cols_ref, rows_ref, shift_ref, flip_ref, sems
):
    fetch = [
        pltpu.make_async_copy(shift_in, shift_ref, sems.at[0]),
        pltpu.make_async_copy(flip_in, flip_ref, sems.at[1]),
    ]
    for copy in fetch:
        copy.start()
    square = (ORDER, ORDER)
    sub = lax.broadcasted_iota(jnp.int32, square, 0)
    lane = lax.broadcasted_iota(jnp.int32, square, 1)
    re, im = wave(lane >> 4, lane & 15, sub >> 4, sub & 15)
    cols_ref[2 * TRANS, :ORDER] = re
    cols_ref[2 * TRANS, ORDER:] = im
    re, im = wave(sub >> 4, sub & 15, lane >> 4, lane & 15)
    base = jnp.concatenate([re, im], 1)
    both = lax.broadcasted_iota(jnp.int32, (2 * BAND, ORDER), 0)
    grp = jnp.where(both < BAND, place_ref[0], place_ref[0] ^ 1)
    band_row = (both & (BAND - 1)) + grp * BAND
    band_lane = lax.broadcasted_iota(jnp.int32, (2 * BAND, ORDER), 1)

    def put_rows(slot, target):
        pick = jnp.where(band_lane == target, 1.0, 0.0).astype(BF)
        out = jnp.dot(pick, base, preferred_element_type=F32).astype(BF)
        for b in range(2):
            part = out[BAND * b : BAND * (b + 1)]
            rows_ref[b, 2 * BAND * slot : 2 * BAND * slot + BAND] = part[:, :ORDER]
            rows_ref[b, 2 * BAND * slot + BAND : 2 * BAND * (slot + 1)] = part[:, ORDER:]

    def put_cols(slot, target):
        pick = jnp.where(sub == target, 1.0, 0.0).astype(BF)
        cols_ref[slot] = jnp.dot(cols_ref[2 * TRANS], pick, preferred_element_type=F32).astype(BF)

    put_rows(0, band_row)
    for copy in fetch:
        copy.wait()
    for t in range(TRANS):
        freq, mom = shift_ref[t, 0] >> 4, shift_ref[t, 0] & 15

        def moved(i, freq=freq, mom=mom):
            return ((((i >> 4) + freq) & 15) << 4) + (((i & 15) + mom) & 15)

        put_rows(1 + t, moved(band_row))
        put_cols(t, moved(lane))
        freq, mom = flip_ref[t, 0] >> 4, flip_ref[t, 0] & 15

        def turned(i, freq=freq, mom=mom):
            return (((freq - (i >> 4)) & 15) << 4) + ((mom - (i & 15)) & 15)

        put_rows(1 + TRANS + t, turned(band_row))
        put_cols(TRANS + t, turned(lane))


def tables(place, shift, flip):
    return pl.pallas_call(
        table_kernel,
        out_shape=(
            jax.ShapeDtypeStruct((2 * TRANS + 1, 2 * ORDER, ORDER), BF),
            jax.ShapeDtypeStruct((2, (2 * TRANS + 1) * 2 * BAND, ORDER), BF),
        ),
        in_specs=[
            pl.BlockSpec(memory_space=pltpu.SMEM),
            pl.BlockSpec(memory_space=pltpu.HBM),
            pl.BlockSpec(memory_space=pltpu.HBM),
        ],
        out_specs=(pl.BlockSpec(memory_space=pltpu.VMEM),) * 2,
        scratch_shapes=[
            pltpu.SMEM((TRANS, ORDER), jnp.int32),
            pltpu.SMEM((TRANS, ORDER), jnp.int32),
            pltpu.SemaphoreType.DMA((2,)),
        ],
        cost_estimate=pl.CostEstimate(flops=4 * 10**9, bytes_accessed=1, transcendentals=0),
        compiler_params=pltpu.CompilerParams(vmem_limit_bytes=12 * MIB),
        name="tables",
    )(place, shift, flip)


def paired(re, im):
    return jnp.concatenate(
        [jnp.concatenate([re, im], 1), jnp.concatenate([im, -re], 1)], 0
    )


def halves(ref, begin):
    return paired(ref[begin : begin + BAND], ref[begin + BAND : begin + 2 * BAND])


def one_walker(up, down, cols, rows, first_up, first_down, plain, ready, put):
    step = 2 * BAND
    first_up[...] = jnp.dot(rows[: step * (TRANS + 1)], up, preferred_element_type=F32).astype(BF)
    first_down[...] = jnp.dot(rows[step:], down, preferred_element_type=F32).astype(BF)
    across = (((1,), (1,)), ((), ()))
    turned_up = lax.dot_general(rows[:step], up, across, preferred_element_type=F32).astype(BF)
    turned_down = lax.dot_general(rows[:step], down, across, preferred_element_type=F32).astype(BF)
    left = jnp.concatenate(
        [halves(turned_up, 0), halves(turned_down, 0), halves(first_up, 0)], 0
    )
    plain[...] = jnp.dot(left, cols[2 * TRANS], preferred_element_type=F32)
    ready()
    for t in range(TRANS):
        left = jnp.concatenate([halves(first_up, step * (1 + t)), halves(first_down, step * t)], 0)
        moved = jnp.dot(left, cols[t], preferred_element_type=F32)
        real, imag = 0.0, 0.0
        for s in range(2):
            nr, ni = plain[step * s : step * s + BAND], plain[step * s + BAND : step * (s + 1)]
            mr, mi = moved[step * s : step * s + BAND], moved[step * s + BAND : step * (s + 1)]
            real = real + (nr * mr + ni * mi)
            imag = imag + (nr * mi - ni * mr)
        put(0, 0, t, real)
        put(0, 1, t, imag)
        low = jnp.dot(
            halves(first_down, step * (TRANS + t)), cols[TRANS + t], preferred_element_type=F32
        )
        nr, ni = plain[2 * step : 2 * step + BAND], plain[2 * step + BAND : 3 * step]
        put(1, 0, t, nr * low[:BAND] - ni * low[BAND:])
        put(1, 1, t, nr * low[BAND:] + ni * low[:BAND])


WORK = [
    pltpu.VMEM((2 * BAND * (TRANS + 1), ORDER), BF),
    pltpu.VMEM((2 * BAND * 2 * TRANS, ORDER), BF),
    pltpu.VMEM((6 * BAND, ORDER), F32),
]
SUMS = (2, TRANS, BAND, ORDER)
PIECE = (2, ORDER, ORDER)
IN_VMEM = pl.BlockSpec(memory_space=pltpu.VMEM)
IN_SMEM = pl.BlockSpec(memory_space=pltpu.SMEM)
ANYWHERE = pl.BlockSpec(memory_space=pl.ANY)
IN_HBM = pl.BlockSpec(memory_space=pltpu.HBM)
BIG = pltpu.CompilerParams(vmem_limit_bytes=16 * MIB)


def open_kernel(
    piece, cols, rows, ph_in, pp_in, sums, kept, first_up, first_down, plain, sems
):
    loads = [
        pltpu.make_async_copy(source.at[part], sums.at[i, part], sems.at[i, part])
        for i, source in enumerate((ph_in, pp_in))
        for part in range(2)
    ]
    for load in loads:
        load.start()

    def ready():
        for load in loads:
            load.wait()

    def put(which, part, t, term):
        sums[which, part, t] += term

    one_walker(piece[0], piece[1], cols, rows.at[0], first_up, first_down, plain, ready, put)
    kept[...] = piece[...]


def open_sums(piece, cols, rows, ph, pp):
    return pl.pallas_call(
        open_kernel,
        out_shape=(jax.ShapeDtypeStruct((2, *SUMS), F32), jax.ShapeDtypeStruct(PIECE, BF)),
        in_specs=[IN_VMEM] * 3 + [IN_HBM] * 2,
        out_specs=(IN_VMEM,) * 2,
        scratch_shapes=WORK + [pltpu.SemaphoreType.DMA((2, 2))],
        cost_estimate=pl.CostEstimate(flops=4 * 10**9, bytes_accessed=1, transcendentals=0),
        compiler_params=BIG,
        name="open_sums",
    )(piece, cols, rows, ph, pp)


def spread_kernel(count, fresh, send, *refs):
    pieces = refs[:count]
    cols, rows, before = refs[count : count + 3]
    after = refs[count + 3 : count + 4 + send]
    first_up, first_down, plain, *held = refs[count + 4 + send :]
    for n, piece in enumerate(pieces):
        for b in range(2):

            def put(which, part, t, term, n=n, b=b):
                if n == 0:
                    if not (fresh and b):
                        term = term + before[2 * b + which, part, t]
                elif send and b:
                    term = term + held[0][which, part, t]
                else:
                    term = term + after[0][2 * b + which, part, t]
                if not (send and b):
                    after[0][2 * b + which, part, t] = term
                elif n < count - 1:
                    held[0][which, part, t] = term
                else:
                    after[1][which, part, t] = term.astype(BF)

            one_walker(
                piece[0], piece[1], cols, rows.at[b], first_up, first_down, plain,
                lambda: None, put,
            )


def spread(pieces, cols, rows, sums, send=False):
    count, fresh = len(pieces), sums.shape[0] == 2
    out_shape = [jax.ShapeDtypeStruct((2 if send else 4, *SUMS), F32)]
    if send:
        out_shape.append(jax.ShapeDtypeStruct((2, *SUMS), BF))
    return pl.pallas_call(
        functools.partial(spread_kernel, count, fresh, send),
        out_shape=tuple(out_shape),
        in_specs=[IN_VMEM] * (count + 3),
        out_specs=(IN_VMEM,) * len(out_shape),
        scratch_shapes=WORK + [pltpu.VMEM((2, *SUMS), F32)] * send,
        cost_estimate=TINY,
        compiler_params=BIG,
        name="spread",
    )(*pieces, cols, rows, sums)


def add_kernel(piece, cols, rows, before, after, first_up, first_down, plain):
    def put(which, part, t, term):
        after[which, part, t] = before[which, part, t] + term

    one_walker(
        piece[0], piece[1], cols, rows.at[0], first_up, first_down, plain, lambda: None, put
    )


def add(piece, cols, rows, sums):
    return pl.pallas_call(
        add_kernel,
        out_shape=jax.ShapeDtypeStruct((2, *SUMS), F32),
        in_specs=[IN_VMEM] * 4,
        out_specs=IN_VMEM,
        scratch_shapes=WORK,
        cost_estimate=TINY,
        compiler_params=BIG,
        name="add",
    )(piece, cols, rows, sums)


def close_kernel(
    piece, cols, rows, sums, others, ph, pp, first_up, first_down, plain, total, sems
):
    stores = []

    def put(which, part, t, term):
        other = others[which, part, t].astype(F32)
        total[which, part, t] = sums[which, part, t] + other + term
        store = pltpu.make_async_copy(
            total.at[which, part, t], (ph, pp)[which].at[part, t], sems.at[which, part, t]
        )
        store.start()
        stores.append(store)

    one_walker(
        piece[0], piece[1], cols, rows.at[0], first_up, first_down, plain, lambda: None, put
    )
    for store in stores:
        store.wait()


def close_sums(piece, cols, rows, sums, others):
    return pl.pallas_call(
        close_kernel,
        out_shape=(jax.ShapeDtypeStruct(SUMS, F32),) * 2,
        in_specs=[IN_VMEM] * 5,
        out_specs=(ANYWHERE,) * 2,
        scratch_shapes=WORK
        + [pltpu.VMEM((2, *SUMS), F32), pltpu.SemaphoreType.DMA((2, 2, TRANS))],
        cost_estimate=TINY,
        compiler_params=BIG,
        name="close_sums",
    )(piece, cols, rows, sums, others)


def scale_kernel(masses, spins, out):
    signed = (2 * spins[...] - 1).astype(F32)
    for spin, sign in enumerate((COUPLING, -COUPLING)):
        out[spin] = (masses[0, spin].astype(F32) * jnp.exp(sign * signed)).astype(BF)


def scale(masses, spins):
    return pl.pallas_call(
        scale_kernel,
        out_shape=jax.ShapeDtypeStruct(PIECE, BF),
        in_specs=[IN_VMEM] * 2,
        out_specs=IN_VMEM,
        cost_estimate=TINY,
        compiler_params=pltpu.CompilerParams(vmem_limit_bytes=56 * MIB),
        name="scale",
    )(masses, spins)


def route_kernel(steps, place, y_ref, own, got, *refs):
    outs, sems = refs[: len(steps)], refs[len(steps)]
    for i, step in enumerate(steps):
        wraps = (place[0] & 1 == 0) | (y_ref[0] + step >= PLANE)

        @pl.when(wraps)
        def _(i=i):
            pltpu.make_async_copy(got, outs[i], sems.at[i]).start()

        @pl.when(jnp.logical_not(wraps))
        def _(i=i):
            pltpu.make_async_copy(own, outs[i], sems.at[i]).start()

    for i in range(len(steps)):
        pltpu.make_async_copy(own, outs[i], sems.at[i]).wait()


def route(place, y, own, got, steps):
    return pl.pallas_call(
        functools.partial(route_kernel, steps),
        out_shape=(jax.ShapeDtypeStruct(own.shape, BF),) * len(steps),
        in_specs=[IN_SMEM] * 2 + [ANYWHERE] * 2,
        out_specs=(ANYWHERE,) * len(steps),
        scratch_shapes=[pltpu.SemaphoreType.DMA((len(steps),))],
        cost_estimate=TINY,
        compiler_params=pltpu.CompilerParams(vmem_limit_bytes=MIB),
        name="route",
    )(place, y, own, got)


PLANE = 4
BLOCKS = 64


def planes_back(value):
    pairs = [
        (g * BLOCKS + b, g * BLOCKS + (b + PLANE * (1 + g % 2)) % BLOCKS)
        for g in range(4)
        for b in range(BLOCKS)
    ]
    return lax.ppermute(value, ("grp", "blk"), pairs)


def along_y(value, steps):
    pairs = [(b, b // PLANE * PLANE + (b + steps) % PLANE) for b in range(BLOCKS)]
    return lax.ppermute(value, "blk", pairs)


def other_core(value):
    return lax.ppermute(value, "grp", [(s, s ^ 1) for s in range(4)])


def on_device(masses, spins, shift_table, flip_table, ph_in, pp_in):
    place = lax.axis_index("grp").reshape(1).astype(jnp.int32)
    y = (lax.axis_index("blk") % PLANE).reshape(1).astype(jnp.int32)
    own = scale(masses, spins)
    got = planes_back(own)
    cols, rows = tables(place, shift_table, flip_table)
    sums, kept = open_sums(own, cols, rows, ph_in, pp_in)
    right, left, middle = route(place, y, kept, got, (1, 3, 2))
    right, left = along_y(right, 1), along_y(left, 3)
    (sums,) = spread([got], cols, rows, sums)
    middle, sums = lax.optimization_barrier((middle, sums))
    middle = along_y(middle, 2)
    right, left, sums = lax.optimization_barrier((right, left, sums))
    sums, sent = spread([right, left], cols, rows, sums, True)
    others = other_core(sent)
    middle, sums = lax.optimization_barrier((middle, sums))
    swapped = other_core(middle)
    sums = add(middle, cols, rows, sums)
    return close_sums(swapped, cols, rows, sums, others)


def solution(mesh):
    placed = (
        P("blk", None, None, None),
        P("blk", None),
        P("blk", None),
        P("blk", None),
        P(None, "blk", "grp", None),
        P(None, "blk", "grp", None),
    )
    return jax.shard_map(
        on_device,
        mesh=mesh,
        in_specs=placed,
        out_specs=(P(None, "blk", "grp", None), P(None, "blk", "grp", None)),
        check_vma=False,
    )
```

```python
import functools
import math

import jax
import jax.numpy as jnp
from jax import lax
from jax.experimental import pallas as pl
from jax.experimental.pallas import tpu as pltpu
from jax.sharding import PartitionSpec as P

NK = 16
ORDER = 256
BAND = 64
TRANS = 4
COUPLING = 0.5
BF = jnp.bfloat16
F32 = jnp.float32
MIB = 1 << 20
TINY = pl.CostEstimate(flops=1, bytes_accessed=1, transcendentals=0)


def wave(freq, mom, tau, site):
    turns = ((2 * freq + 1) * tau - 2 * mom * site) & 31
    phase = turns.astype(F32) * (math.pi / 16.0)
    return (jnp.cos(phase) * 0.0625).astype(BF), (jnp.sin(phase) * 0.0625).astype(BF)


def table_kernel(
    place_ref, shift_in, flip_in, cols_ref, rows_ref, shift_ref, flip_ref, sems
):
    fetch = [
        pltpu.make_async_copy(shift_in, shift_ref, sems.at[0]),
        pltpu.make_async_copy(flip_in, flip_ref, sems.at[1]),
    ]
    for copy in fetch:
        copy.start()
    square = (ORDER, ORDER)
    sub = lax.broadcasted_iota(jnp.int32, square, 0)
    lane = lax.broadcasted_iota(jnp.int32, square, 1)
    re, im = wave(lane >> 4, lane & 15, sub >> 4, sub & 15)
    cols_ref[2 * TRANS, :ORDER] = re
    cols_ref[2 * TRANS, ORDER:] = im
    re, im = wave(sub >> 4, sub & 15, lane >> 4, lane & 15)
    base = jnp.concatenate([re, im], 1)
    both = lax.broadcasted_iota(jnp.int32, (2 * BAND, ORDER), 0)
    grp = jnp.where(both < BAND, place_ref[0], place_ref[0] ^ 1)
    band_row = (both & (BAND - 1)) + grp * BAND
    band_lane = lax.broadcasted_iota(jnp.int32, (2 * BAND, ORDER), 1)

    def put_rows(slot, target):
        pick = jnp.where(band_lane == target, 1.0, 0.0).astype(BF)
        out = jnp.dot(pick, base, preferred_element_type=F32).astype(BF)
        for b in range(2):
            part = out[BAND * b : BAND * (b + 1)]
            rows_ref[b, 2 * BAND * slot : 2 * BAND * slot + BAND] = part[:, :ORDER]
            rows_ref[b, 2 * BAND * slot + BAND : 2 * BAND * (slot + 1)] = part[:, ORDER:]

    def put_cols(slot, target):
        pick = jnp.where(sub == target, 1.0, 0.0).astype(BF)
        cols_ref[slot] = jnp.dot(cols_ref[2 * TRANS], pick, preferred_element_type=F32).astype(BF)

    put_rows(0, band_row)
    for copy in fetch:
        copy.wait()
    for t in range(TRANS):
        freq, mom = shift_ref[t, 0] >> 4, shift_ref[t, 0] & 15

        def moved(i, freq=freq, mom=mom):
            return ((((i >> 4) + freq) & 15) << 4) + (((i & 15) + mom) & 15)

        put_rows(1 + t, moved(band_row))
        put_cols(t, moved(lane))
        freq, mom = flip_ref[t, 0] >> 4, flip_ref[t, 0] & 15

        def turned(i, freq=freq, mom=mom):
            return (((freq - (i >> 4)) & 15) << 4) + ((mom - (i & 15)) & 15)

        put_rows(1 + TRANS + t, turned(band_row))
        put_cols(TRANS + t, turned(lane))


def tables(place, shift, flip):
    return pl.pallas_call(
        table_kernel,
        out_shape=(
            jax.ShapeDtypeStruct((2 * TRANS + 1, 2 * ORDER, ORDER), BF),
            jax.ShapeDtypeStruct((2, (2 * TRANS + 1) * 2 * BAND, ORDER), BF),
        ),
        in_specs=[
            pl.BlockSpec(memory_space=pltpu.SMEM),
            pl.BlockSpec(memory_space=pltpu.HBM),
            pl.BlockSpec(memory_space=pltpu.HBM),
        ],
        out_specs=(pl.BlockSpec(memory_space=pltpu.VMEM),) * 2,
        scratch_shapes=[
            pltpu.SMEM((TRANS, ORDER), jnp.int32),
            pltpu.SMEM((TRANS, ORDER), jnp.int32),
            pltpu.SemaphoreType.DMA((2,)),
        ],
        cost_estimate=pl.CostEstimate(flops=4 * 10**9, bytes_accessed=1, transcendentals=0),
        compiler_params=pltpu.CompilerParams(vmem_limit_bytes=12 * MIB),
        name="tables",
    )(place, shift, flip)


def paired(re, im):
    return jnp.concatenate(
        [jnp.concatenate([re, im], 1), jnp.concatenate([im, -re], 1)], 0
    )


def halves(ref, begin):
    return paired(ref[begin : begin + BAND], ref[begin + BAND : begin + 2 * BAND])


def one_walker(up, down, cols, rows, first_up, first_down, plain, ready, put):
    step = 2 * BAND
    first_up[...] = jnp.dot(rows[: step * (TRANS + 1)], up, preferred_element_type=F32).astype(BF)
    first_down[...] = jnp.dot(rows[step:], down, preferred_element_type=F32).astype(BF)
    across = (((1,), (1,)), ((), ()))
    turned_up = lax.dot_general(rows[:step], up, across, preferred_element_type=F32).astype(BF)
    turned_down = lax.dot_general(rows[:step], down, across, preferred_element_type=F32).astype(BF)
    left = jnp.concatenate(
        [halves(turned_up, 0), halves(turned_down, 0), halves(first_up, 0)], 0
    )
    plain[...] = jnp.dot(left, cols[2 * TRANS], preferred_element_type=F32)
    ready()
    for t in range(TRANS):
        left = jnp.concatenate([halves(first_up, step * (1 + t)), halves(first_down, step * t)], 0)
        moved = jnp.dot(left, cols[t], preferred_element_type=F32)
        real, imag = 0.0, 0.0
        for s in range(2):
            nr, ni = plain[step * s : step * s + BAND], plain[step * s + BAND : step * (s + 1)]
            mr, mi = moved[step * s : step * s + BAND], moved[step * s + BAND : step * (s + 1)]
            real = real + (nr * mr + ni * mi)
            imag = imag + (nr * mi - ni * mr)
        put(0, 0, t, real)
        put(0, 1, t, imag)
        low = jnp.dot(
            halves(first_down, step * (TRANS + t)), cols[TRANS + t], preferred_element_type=F32
        )
        nr, ni = plain[2 * step : 2 * step + BAND], plain[2 * step + BAND : 3 * step]
        put(1, 0, t, nr * low[:BAND] - ni * low[BAND:])
        put(1, 1, t, nr * low[BAND:] + ni * low[:BAND])


WORK = [
    pltpu.VMEM((2 * BAND * (TRANS + 1), ORDER), BF),
    pltpu.VMEM((2 * BAND * 2 * TRANS, ORDER), BF),
    pltpu.VMEM((6 * BAND, ORDER), F32),
]
SUMS = (2, TRANS, BAND, ORDER)
PIECE = (2, ORDER, ORDER)
IN_VMEM = pl.BlockSpec(memory_space=pltpu.VMEM)
IN_SMEM = pl.BlockSpec(memory_space=pltpu.SMEM)
ANYWHERE = pl.BlockSpec(memory_space=pl.ANY)
IN_HBM = pl.BlockSpec(memory_space=pltpu.HBM)
BIG = pltpu.CompilerParams(vmem_limit_bytes=16 * MIB)


def open_kernel(
    piece, cols, rows, ph_in, pp_in, sums, kept, first_up, first_down, plain, sems
):
    loads = [
        pltpu.make_async_copy(source.at[part], sums.at[i, part], sems.at[i, part])
        for i, source in enumerate((ph_in, pp_in))
        for part in range(2)
    ]
    for load in loads:
        load.start()

    def ready():
        for load in loads:
            load.wait()

    def put(which, part, t, term):
        sums[which, part, t] += term

    one_walker(piece[0], piece[1], cols, rows.at[0], first_up, first_down, plain, ready, put)
    kept[...] = piece[...]


def open_sums(piece, cols, rows, ph, pp):
    return pl.pallas_call(
        open_kernel,
        out_shape=(jax.ShapeDtypeStruct((2, *SUMS), F32), jax.ShapeDtypeStruct(PIECE, BF)),
        in_specs=[IN_VMEM] * 3 + [IN_HBM] * 2,
        out_specs=(IN_VMEM,) * 2,
        scratch_shapes=WORK + [pltpu.SemaphoreType.DMA((2, 2))],
        cost_estimate=pl.CostEstimate(flops=4 * 10**9, bytes_accessed=1, transcendentals=0),
        compiler_params=BIG,
        name="open_sums",
    )(piece, cols, rows, ph, pp)


def spread_kernel(count, fresh, send, *refs):
    pieces = refs[:count]
    cols, rows, before = refs[count : count + 3]
    after = refs[count + 3 : count + 4 + send]
    first_up, first_down, plain, *held = refs[count + 4 + send :]
    for n, piece in enumerate(pieces):
        for b in range(2):

            def put(which, part, t, term, n=n, b=b):
                if n == 0:
                    if not (fresh and b):
                        term = term + before[2 * b + which, part, t]
                elif send and b:
                    term = term + held[0][which, part, t]
                else:
                    term = term + after[0][2 * b + which, part, t]
                if not (send and b):
                    after[0][2 * b + which, part, t] = term
                elif n < count - 1:
                    held[0][which, part, t] = term
                else:
                    after[1][which, part, t] = term.astype(BF)

            one_walker(
                piece[0], piece[1], cols, rows.at[b], first_up, first_down, plain,
                lambda: None, put,
            )


def spread(pieces, cols, rows, sums, send=False):
    count, fresh = len(pieces), sums.shape[0] == 2
    out_shape = [jax.ShapeDtypeStruct((2 if send else 4, *SUMS), F32)]
    if send:
        out_shape.append(jax.ShapeDtypeStruct((2, *SUMS), BF))
    return pl.pallas_call(
        functools.partial(spread_kernel, count, fresh, send),
        out_shape=tuple(out_shape),
        in_specs=[IN_VMEM] * (count + 3),
        out_specs=(IN_VMEM,) * len(out_shape),
        scratch_shapes=WORK + [pltpu.VMEM((2, *SUMS), F32)] * send,
        cost_estimate=TINY,
        compiler_params=BIG,
        name="spread",
    )(*pieces, cols, rows, sums)


def add_kernel(piece, cols, rows, before, after, first_up, first_down, plain):
    def put(which, part, t, term):
        after[which, part, t] = before[which, part, t] + term

    one_walker(
        piece[0], piece[1], cols, rows.at[0], first_up, first_down, plain, lambda: None, put
    )


def add(piece, cols, rows, sums):
    return pl.pallas_call(
        add_kernel,
        out_shape=jax.ShapeDtypeStruct((2, *SUMS), F32),
        in_specs=[IN_VMEM] * 4,
        out_specs=IN_VMEM,
        scratch_shapes=WORK,
        cost_estimate=TINY,
        compiler_params=BIG,
        name="add",
    )(piece, cols, rows, sums)


def close_kernel(
    piece, cols, rows, sums, others, ph, pp, first_up, first_down, plain, total, sems
):
    stores = []

    def put(which, part, t, term):
        other = others[which, part, t].astype(F32)
        total[which, part, t] = sums[which, part, t] + other + term
        store = pltpu.make_async_copy(
            total.at[which, part, t], (ph, pp)[which].at[part, t], sems.at[which, part, t]
        )
        store.start()
        stores.append(store)

    one_walker(
        piece[0], piece[1], cols, rows.at[0], first_up, first_down, plain, lambda: None, put
    )
    for store in stores:
        store.wait()


def close_sums(piece, cols, rows, sums, others):
    return pl.pallas_call(
        close_kernel,
        out_shape=(jax.ShapeDtypeStruct(SUMS, F32),) * 2,
        in_specs=[IN_VMEM] * 5,
        out_specs=(ANYWHERE,) * 2,
        scratch_shapes=WORK
        + [pltpu.VMEM((2, *SUMS), F32), pltpu.SemaphoreType.DMA((2, 2, TRANS))],
        cost_estimate=TINY,
        compiler_params=BIG,
        name="close_sums",
    )(piece, cols, rows, sums, others)


def scale_kernel(masses, spins, out):
    signed = (2 * spins[...] - 1).astype(F32)
    for spin, sign in enumerate((COUPLING, -COUPLING)):
        out[spin] = (masses[0, spin].astype(F32) * jnp.exp(sign * signed)).astype(BF)


def scale(masses, spins):
    return pl.pallas_call(
        scale_kernel,
        out_shape=jax.ShapeDtypeStruct(PIECE, BF),
        in_specs=[IN_VMEM] * 2,
        out_specs=IN_VMEM,
        cost_estimate=TINY,
        compiler_params=pltpu.CompilerParams(vmem_limit_bytes=56 * MIB),
        name="scale",
    )(masses, spins)


def route_kernel(steps, place, y_ref, own, got, *refs):
    outs, sems = refs[: len(steps)], refs[len(steps)]
    for i, step in enumerate(steps):
        wraps = (place[0] & 1 == 0) | (y_ref[0] + step >= PLANE)

        @pl.when(wraps)
        def _(i=i):
            pltpu.make_async_copy(got, outs[i], sems.at[i]).start()

        @pl.when(jnp.logical_not(wraps))
        def _(i=i):
            pltpu.make_async_copy(own, outs[i], sems.at[i]).start()

    for i in range(len(steps)):
        pltpu.make_async_copy(own, outs[i], sems.at[i]).wait()


def route(place, y, own, got, steps):
    return pl.pallas_call(
        functools.partial(route_kernel, steps),
        out_shape=(jax.ShapeDtypeStruct(own.shape, BF),) * len(steps),
        in_specs=[IN_SMEM] * 2 + [ANYWHERE] * 2,
        out_specs=(ANYWHERE,) * len(steps),
        scratch_shapes=[pltpu.SemaphoreType.DMA((len(steps),))],
        cost_estimate=TINY,
        compiler_params=pltpu.CompilerParams(vmem_limit_bytes=MIB),
        name="route",
    )(place, y, own, got)


PLANE = 4
BLOCKS = 64


def planes_back(value):
    pairs = [
        (g * BLOCKS + b, g * BLOCKS + (b + PLANE * (1 + g % 2)) % BLOCKS)
        for g in range(4)
        for b in range(BLOCKS)
    ]
    return lax.ppermute(value, ("grp", "blk"), pairs)


def along_y(value, steps):
    pairs = [(b, b // PLANE * PLANE + (b + steps) % PLANE) for b in range(BLOCKS)]
    return lax.ppermute(value, "blk", pairs)


def other_core(value):
    return lax.ppermute(value, "grp", [(s, s ^ 1) for s in range(4)])


def on_device(masses, spins, shift_table, flip_table, ph_in, pp_in):
    place = lax.axis_index("grp").reshape(1).astype(jnp.int32)
    y = (lax.axis_index("blk") % PLANE).reshape(1).astype(jnp.int32)
    own = scale(masses, spins)
    got = planes_back(own)
    cols, rows = tables(place, shift_table, flip_table)
    sums, kept = open_sums(own, cols, rows, ph_in, pp_in)
    right, left, middle = route(place, y, kept, got, (1, 3, 2))
    right, left = along_y(right, 1), along_y(left, 3)
    (sums,) = spread([got], cols, rows, sums)
    middle, sums = lax.optimization_barrier((middle, sums))
    middle = along_y(middle, 2)
    right, sums = lax.optimization_barrier((right, sums))
    (sums,) = spread([right], cols, rows, sums)
    left, sums = lax.optimization_barrier((left, sums))
    sums, sent = spread([left], cols, rows, sums, True)
    others = other_core(sent)
    middle, sums = lax.optimization_barrier((middle, sums))
    swapped = other_core(middle)
    sums = add(middle, cols, rows, sums)
    return close_sums(swapped, cols, rows, sums, others)


def solution(mesh):
    placed = (
        P("blk", None, None, None),
        P("blk", None),
        P("blk", None),
        P("blk", None),
        P(None, "blk", "grp", None),
        P(None, "blk", "grp", None),
    )
    return jax.shard_map(
        on_device,
        mesh=mesh,
        in_specs=placed,
        out_specs=(P(None, "blk", "grp", None), P(None, "blk", "grp", None)),
        check_vma=False,
    )
```

```python
import functools
import math

import jax
import jax.numpy as jnp
from jax import lax
from jax.experimental import pallas as pl
from jax.experimental.pallas import tpu as pltpu
from jax.sharding import PartitionSpec as P

NK = 16
ORDER = 256
BAND = 64
TRANS = 4
COUPLING = 0.5
BF = jnp.bfloat16
F32 = jnp.float32
MIB = 1 << 20
TINY = pl.CostEstimate(flops=1, bytes_accessed=1, transcendentals=0)


def wave(freq, mom, tau, site):
    turns = ((2 * freq + 1) * tau - 2 * mom * site) & 31
    phase = turns.astype(F32) * (math.pi / 16.0)
    return (jnp.cos(phase) * 0.0625).astype(BF), (jnp.sin(phase) * 0.0625).astype(BF)


def table_kernel(
    place_ref, shift_in, flip_in, cols_ref, rows_ref, shift_ref, flip_ref, sems
):
    fetch = [
        pltpu.make_async_copy(shift_in, shift_ref, sems.at[0]),
        pltpu.make_async_copy(flip_in, flip_ref, sems.at[1]),
    ]
    for copy in fetch:
        copy.start()
    square = (ORDER, ORDER)
    sub = lax.broadcasted_iota(jnp.int32, square, 0)
    lane = lax.broadcasted_iota(jnp.int32, square, 1)
    re, im = wave(lane >> 4, lane & 15, sub >> 4, sub & 15)
    cols_ref[2 * TRANS, :ORDER] = re
    cols_ref[2 * TRANS, ORDER:] = im
    re, im = wave(sub >> 4, sub & 15, lane >> 4, lane & 15)
    base = jnp.concatenate([re, im], 1)
    both = lax.broadcasted_iota(jnp.int32, (2 * BAND, ORDER), 0)
    grp = jnp.where(both < BAND, place_ref[0], place_ref[0] ^ 1)
    band_row = (both & (BAND - 1)) + grp * BAND
    band_lane = lax.broadcasted_iota(jnp.int32, (2 * BAND, ORDER), 1)

    def put_rows(slot, target):
        pick = jnp.where(band_lane == target, 1.0, 0.0).astype(BF)
        out = jnp.dot(pick, base, preferred_element_type=F32).astype(BF)
        for b in range(2):
            part = out[BAND * b : BAND * (b + 1)]
            rows_ref[b, 2 * BAND * slot : 2 * BAND * slot + BAND] = part[:, :ORDER]
            rows_ref[b, 2 * BAND * slot + BAND : 2 * BAND * (slot + 1)] = part[:, ORDER:]

    def put_cols(slot, target):
        pick = jnp.where(sub == target, 1.0, 0.0).astype(BF)
        cols_ref[slot] = jnp.dot(cols_ref[2 * TRANS], pick, preferred_element_type=F32).astype(BF)

    put_rows(0, band_row)
    for copy in fetch:
        copy.wait()
    for t in range(TRANS):
        freq, mom = shift_ref[t, 0] >> 4, shift_ref[t, 0] & 15

        def moved(i, freq=freq, mom=mom):
            return ((((i >> 4) + freq) & 15) << 4) + (((i & 15) + mom) & 15)

        put_rows(1 + t, moved(band_row))
        put_cols(t, moved(lane))
        freq, mom = flip_ref[t, 0] >> 4, flip_ref[t, 0] & 15

        def turned(i, freq=freq, mom=mom):
            return (((freq - (i >> 4)) & 15) << 4) + ((mom - (i & 15)) & 15)

        put_rows(1 + TRANS + t, turned(band_row))
        put_cols(TRANS + t, turned(lane))


def tables(place, shift, flip):
    return pl.pallas_call(
        table_kernel,
        out_shape=(
            jax.ShapeDtypeStruct((2 * TRANS + 1, 2 * ORDER, ORDER), BF),
            jax.ShapeDtypeStruct((2, (2 * TRANS + 1) * 2 * BAND, ORDER), BF),
        ),
        in_specs=[
            pl.BlockSpec(memory_space=pltpu.SMEM),
            pl.BlockSpec(memory_space=pltpu.HBM),
            pl.BlockSpec(memory_space=pltpu.HBM),
        ],
        out_specs=(pl.BlockSpec(memory_space=pltpu.VMEM),) * 2,
        scratch_shapes=[
            pltpu.SMEM((TRANS, ORDER), jnp.int32),
            pltpu.SMEM((TRANS, ORDER), jnp.int32),
            pltpu.SemaphoreType.DMA((2,)),
        ],
        cost_estimate=pl.CostEstimate(flops=4 * 10**9, bytes_accessed=1, transcendentals=0),
        compiler_params=pltpu.CompilerParams(vmem_limit_bytes=12 * MIB),
        name="tables",
    )(place, shift, flip)


def paired(re, im):
    return jnp.concatenate(
        [jnp.concatenate([re, im], 1), jnp.concatenate([im, -re], 1)], 0
    )


def halves(ref, begin):
    return paired(ref[begin : begin + BAND], ref[begin + BAND : begin + 2 * BAND])


def one_walker(up, down, cols, rows, first_up, first_down, plain, ready, put):
    step = 2 * BAND
    first_up[...] = jnp.dot(rows[: step * (TRANS + 1)], up, preferred_element_type=F32).astype(BF)
    first_down[...] = jnp.dot(rows[step:], down, preferred_element_type=F32).astype(BF)
    across = (((1,), (1,)), ((), ()))
    turned_up = lax.dot_general(rows[:step], up, across, preferred_element_type=F32).astype(BF)
    turned_down = lax.dot_general(rows[:step], down, across, preferred_element_type=F32).astype(BF)
    left = jnp.concatenate(
        [halves(turned_up, 0), halves(turned_down, 0), halves(first_up, 0)], 0
    )
    plain[...] = jnp.dot(left, cols[2 * TRANS], preferred_element_type=F32)
    ready()
    for t in range(TRANS):
        left = jnp.concatenate([halves(first_up, step * (1 + t)), halves(first_down, step * t)], 0)
        moved = jnp.dot(left, cols[t], preferred_element_type=F32)
        real, imag = 0.0, 0.0
        for s in range(2):
            nr, ni = plain[step * s : step * s + BAND], plain[step * s + BAND : step * (s + 1)]
            mr, mi = moved[step * s : step * s + BAND], moved[step * s + BAND : step * (s + 1)]
            real = real + (nr * mr + ni * mi)
            imag = imag + (nr * mi - ni * mr)
        put(0, 0, t, real)
        put(0, 1, t, imag)
        low = jnp.dot(
            halves(first_down, step * (TRANS + t)), cols[TRANS + t], preferred_element_type=F32
        )
        nr, ni = plain[2 * step : 2 * step + BAND], plain[2 * step + BAND : 3 * step]
        put(1, 0, t, nr * low[:BAND] - ni * low[BAND:])
        put(1, 1, t, nr * low[BAND:] + ni * low[:BAND])


WORK = [
    pltpu.VMEM((2 * BAND * (TRANS + 1), ORDER), BF),
    pltpu.VMEM((2 * BAND * 2 * TRANS, ORDER), BF),
    pltpu.VMEM((6 * BAND, ORDER), F32),
]
SUMS = (2, TRANS, BAND, ORDER)
PIECE = (2, ORDER, ORDER)
IN_VMEM = pl.BlockSpec(memory_space=pltpu.VMEM)
IN_SMEM = pl.BlockSpec(memory_space=pltpu.SMEM)
ANYWHERE = pl.BlockSpec(memory_space=pl.ANY)
IN_HBM = pl.BlockSpec(memory_space=pltpu.HBM)
BIG = pltpu.CompilerParams(vmem_limit_bytes=16 * MIB)


def open_kernel(
    piece, cols, rows, ph_in, pp_in, sums, kept, first_up, first_down, plain, sems
):
    loads = [
        pltpu.make_async_copy(source.at[part], sums.at[i, part], sems.at[i, part])
        for i, source in enumerate((ph_in, pp_in))
        for part in range(2)
    ]
    for load in loads:
        load.start()

    def ready():
        for load in loads:
            load.wait()

    def put(which, part, t, term):
        sums[which, part, t] += term

    one_walker(piece[0], piece[1], cols, rows.at[0], first_up, first_down, plain, ready, put)
    kept[...] = piece[...]


def open_sums(piece, cols, rows, ph, pp):
    return pl.pallas_call(
        open_kernel,
        out_shape=(jax.ShapeDtypeStruct((2, *SUMS), F32), jax.ShapeDtypeStruct(PIECE, BF)),
        in_specs=[IN_VMEM] * 3 + [IN_HBM] * 2,
        out_specs=(IN_VMEM,) * 2,
        scratch_shapes=WORK + [pltpu.SemaphoreType.DMA((2, 2))],
        cost_estimate=pl.CostEstimate(flops=4 * 10**9, bytes_accessed=1, transcendentals=0),
        compiler_params=BIG,
        name="open_sums",
    )(piece, cols, rows, ph, pp)


def spread_kernel(count, fresh, send, *refs):
    pieces = refs[:count]
    cols, rows, before = refs[count : count + 3]
    after = refs[count + 3 : count + 4 + send]
    first_up, first_down, plain, *held = refs[count + 4 + send :]
    for n, piece in enumerate(pieces):
        for b in range(2):

            def put(which, part, t, term, n=n, b=b):
                if n == 0:
                    if not (fresh and b):
                        term = term + before[2 * b + which, part, t]
                elif send and b:
                    term = term + held[0][which, part, t]
                else:
                    term = term + after[0][2 * b + which, part, t]
                if not (send and b):
                    after[0][2 * b + which, part, t] = term
                elif n < count - 1:
                    held[0][which, part, t] = term
                else:
                    after[1][which, part, t] = term.astype(BF)

            one_walker(
                piece[0], piece[1], cols, rows.at[b], first_up, first_down, plain,
                lambda: None, put,
            )


def spread(pieces, cols, rows, sums, send=False):
    count, fresh = len(pieces), sums.shape[0] == 2
    out_shape = [jax.ShapeDtypeStruct((2 if send else 4, *SUMS), F32)]
    if send:
        out_shape.append(jax.ShapeDtypeStruct((2, *SUMS), BF))
    return pl.pallas_call(
        functools.partial(spread_kernel, count, fresh, send),
        out_shape=tuple(out_shape),
        in_specs=[IN_VMEM] * (count + 3),
        out_specs=(IN_VMEM,) * len(out_shape),
        scratch_shapes=WORK + [pltpu.VMEM((2, *SUMS), F32)] * send,
        cost_estimate=TINY,
        compiler_params=BIG,
        name="spread",
    )(*pieces, cols, rows, sums)


def add_kernel(piece, cols, rows, before, after, first_up, first_down, plain):
    def put(which, part, t, term):
        after[which, part, t] = before[which, part, t] + term

    one_walker(
        piece[0], piece[1], cols, rows.at[0], first_up, first_down, plain, lambda: None, put
    )


def add(piece, cols, rows, sums):
    return pl.pallas_call(
        add_kernel,
        out_shape=jax.ShapeDtypeStruct((2, *SUMS), F32),
        in_specs=[IN_VMEM] * 4,
        out_specs=IN_VMEM,
        scratch_shapes=WORK,
        cost_estimate=TINY,
        compiler_params=BIG,
        name="add",
    )(piece, cols, rows, sums)


def close_kernel(
    piece, cols, rows, sums, others, ph, pp, first_up, first_down, plain, total, sems
):
    stores = []

    def put(which, part, t, term):
        other = others[which, part, t].astype(F32)
        total[which, part, t] = sums[which, part, t] + other + term
        store = pltpu.make_async_copy(
            total.at[which, part, t], (ph, pp)[which].at[part, t], sems.at[which, part, t]
        )
        store.start()
        stores.append(store)

    one_walker(
        piece[0], piece[1], cols, rows.at[0], first_up, first_down, plain, lambda: None, put
    )
    for store in stores:
        store.wait()


def close_sums(piece, cols, rows, sums, others):
    return pl.pallas_call(
        close_kernel,
        out_shape=(jax.ShapeDtypeStruct(SUMS, F32),) * 2,
        in_specs=[IN_VMEM] * 5,
        out_specs=(ANYWHERE,) * 2,
        scratch_shapes=WORK
        + [pltpu.VMEM((2, *SUMS), F32), pltpu.SemaphoreType.DMA((2, 2, TRANS))],
        cost_estimate=TINY,
        compiler_params=BIG,
        name="close_sums",
    )(piece, cols, rows, sums, others)


def scale_kernel(masses, spins, out):
    signed = (2 * spins[...] - 1).astype(F32)
    for spin, sign in enumerate((COUPLING, -COUPLING)):
        out[spin] = (masses[0, spin].astype(F32) * jnp.exp(sign * signed)).astype(BF)


def scale(masses, spins):
    return pl.pallas_call(
        scale_kernel,
        out_shape=jax.ShapeDtypeStruct(PIECE, BF),
        in_specs=[IN_VMEM] * 2,
        out_specs=IN_VMEM,
        cost_estimate=TINY,
        compiler_params=pltpu.CompilerParams(vmem_limit_bytes=56 * MIB),
        name="scale",
    )(masses, spins)


def route_kernel(steps, place, y_ref, own, got, *refs):
    outs, sems = refs[: len(steps)], refs[len(steps)]
    for i, step in enumerate(steps):
        wraps = (place[0] & 1 == 0) | (y_ref[0] + step >= PLANE)

        @pl.when(wraps)
        def _(i=i):
            pltpu.make_async_copy(got, outs[i], sems.at[i]).start()

        @pl.when(jnp.logical_not(wraps))
        def _(i=i):
            pltpu.make_async_copy(own, outs[i], sems.at[i]).start()

    for i in range(len(steps)):
        pltpu.make_async_copy(own, outs[i], sems.at[i]).wait()


def route(place, y, own, got, steps):
    return pl.pallas_call(
        functools.partial(route_kernel, steps),
        out_shape=(jax.ShapeDtypeStruct(own.shape, BF),) * len(steps),
        in_specs=[IN_SMEM] * 2 + [ANYWHERE] * 2,
        out_specs=(ANYWHERE,) * len(steps),
        scratch_shapes=[pltpu.SemaphoreType.DMA((len(steps),))],
        cost_estimate=TINY,
        compiler_params=pltpu.CompilerParams(vmem_limit_bytes=MIB),
        name="route",
    )(place, y, own, got)


PLANE = 4
BLOCKS = 64


def planes_back(value):
    pairs = []
    for g in range(4):
        for b in range(BLOCKS):
            target = (b + PLANE * (1 + g % 2)) % BLOCKS
            crosses = target // (BLOCKS // 2) != b // (BLOCKS // 2)
            chip = g ^ 2 if crosses else g
            pairs.append((g * BLOCKS + b, chip * BLOCKS + target))
    return lax.ppermute(value, ("grp", "blk"), pairs)


def along_y(value, steps):
    pairs = [(b, b // PLANE * PLANE + (b + steps) % PLANE) for b in range(BLOCKS)]
    return lax.ppermute(value, "blk", pairs)


def other_core(value):
    return lax.ppermute(value, "grp", [(s, s ^ 1) for s in range(4)])


def on_device(masses, spins, shift_table, flip_table, ph_in, pp_in):
    place = lax.axis_index("grp").reshape(1).astype(jnp.int32)
    y = (lax.axis_index("blk") % PLANE).reshape(1).astype(jnp.int32)
    own = scale(masses, spins)
    got = planes_back(own)
    cols, rows = tables(place, shift_table, flip_table)
    sums, kept = open_sums(own, cols, rows, ph_in, pp_in)
    right, left, middle = route(place, y, kept, got, (1, 3, 2))
    right, left = along_y(right, 1), along_y(left, 3)
    (sums,) = spread([got], cols, rows, sums)
    middle, sums = lax.optimization_barrier((middle, sums))
    middle = along_y(middle, 2)
    right, sums = lax.optimization_barrier((right, sums))
    (sums,) = spread([right], cols, rows, sums)
    left, sums = lax.optimization_barrier((left, sums))
    sums, sent = spread([left], cols, rows, sums, True)
    others = other_core(sent)
    middle, sums = lax.optimization_barrier((middle, sums))
    swapped = other_core(middle)
    sums = add(middle, cols, rows, sums)
    return close_sums(swapped, cols, rows, sums, others)


def solution(mesh):
    placed = (
        P("blk", None, None, None),
        P("blk", None),
        P("blk", None),
        P("blk", None),
        P(None, "blk", "grp", None),
        P(None, "blk", "grp", None),
    )
    return jax.shard_map(
        on_device,
        mesh=mesh,
        in_specs=placed,
        out_specs=(P(None, "blk", "grp", None), P(None, "blk", "grp", None)),
        check_vma=False,
    )
```

```python
import functools
import math

import jax
import jax.numpy as jnp
from jax import lax
from jax.experimental import pallas as pl
from jax.experimental.pallas import tpu as pltpu
from jax.sharding import PartitionSpec as P

NK = 16
ORDER = 256
BAND = 64
TRANS = 4
COUPLING = 0.5
BF = jnp.bfloat16
F32 = jnp.float32
MIB = 1 << 20
TINY = pl.CostEstimate(flops=1, bytes_accessed=1, transcendentals=0)


def wave(freq, mom, tau, site):
    turns = ((2 * freq + 1) * tau - 2 * mom * site) & 31
    phase = turns.astype(F32) * (math.pi / 16.0)
    return (jnp.cos(phase) * 0.0625).astype(BF), (jnp.sin(phase) * 0.0625).astype(BF)


def table_kernel(
    place_ref, shift_in, flip_in, cols_ref, rows_ref, shift_ref, flip_ref, sems
):
    fetch = [
        pltpu.make_async_copy(shift_in, shift_ref, sems.at[0]),
        pltpu.make_async_copy(flip_in, flip_ref, sems.at[1]),
    ]
    for copy in fetch:
        copy.start()
    square = (ORDER, ORDER)
    sub = lax.broadcasted_iota(jnp.int32, square, 0)
    lane = lax.broadcasted_iota(jnp.int32, square, 1)
    re, im = wave(lane >> 4, lane & 15, sub >> 4, sub & 15)
    cols_ref[2 * TRANS, :ORDER] = re
    cols_ref[2 * TRANS, ORDER:] = im
    re, im = wave(sub >> 4, sub & 15, lane >> 4, lane & 15)
    base = jnp.concatenate([re, im], 1)
    both = lax.broadcasted_iota(jnp.int32, (2 * BAND, ORDER), 0)
    grp = jnp.where(both < BAND, place_ref[0], place_ref[0] ^ 1)
    band_row = (both & (BAND - 1)) + grp * BAND
    band_lane = lax.broadcasted_iota(jnp.int32, (2 * BAND, ORDER), 1)

    def put_rows(slot, target):
        pick = jnp.where(band_lane == target, 1.0, 0.0).astype(BF)
        out = jnp.dot(pick, base, preferred_element_type=F32).astype(BF)
        for b in range(2):
            part = out[BAND * b : BAND * (b + 1)]
            rows_ref[b, 2 * BAND * slot : 2 * BAND * slot + BAND] = part[:, :ORDER]
            rows_ref[b, 2 * BAND * slot + BAND : 2 * BAND * (slot + 1)] = part[:, ORDER:]

    def put_cols(slot, target):
        pick = jnp.where(sub == target, 1.0, 0.0).astype(BF)
        cols_ref[slot] = jnp.dot(cols_ref[2 * TRANS], pick, preferred_element_type=F32).astype(BF)

    put_rows(0, band_row)
    for copy in fetch:
        copy.wait()
    for t in range(TRANS):
        freq, mom = shift_ref[t, 0] >> 4, shift_ref[t, 0] & 15

        def moved(i, freq=freq, mom=mom):
            return ((((i >> 4) + freq) & 15) << 4) + (((i & 15) + mom) & 15)

        put_rows(1 + t, moved(band_row))
        put_cols(t, moved(lane))
        freq, mom = flip_ref[t, 0] >> 4, flip_ref[t, 0] & 15

        def turned(i, freq=freq, mom=mom):
            return (((freq - (i >> 4)) & 15) << 4) + ((mom - (i & 15)) & 15)

        put_rows(1 + TRANS + t, turned(band_row))
        put_cols(TRANS + t, turned(lane))


def tables(place, shift, flip):
    return pl.pallas_call(
        table_kernel,
        out_shape=(
            jax.ShapeDtypeStruct((2 * TRANS + 1, 2 * ORDER, ORDER), BF),
            jax.ShapeDtypeStruct((2, (2 * TRANS + 1) * 2 * BAND, ORDER), BF),
        ),
        in_specs=[
            pl.BlockSpec(memory_space=pltpu.SMEM),
            pl.BlockSpec(memory_space=pltpu.HBM),
            pl.BlockSpec(memory_space=pltpu.HBM),
        ],
        out_specs=(pl.BlockSpec(memory_space=pltpu.VMEM),) * 2,
        scratch_shapes=[
            pltpu.SMEM((TRANS, ORDER), jnp.int32),
            pltpu.SMEM((TRANS, ORDER), jnp.int32),
            pltpu.SemaphoreType.DMA((2,)),
        ],
        cost_estimate=pl.CostEstimate(flops=4 * 10**9, bytes_accessed=1, transcendentals=0),
        compiler_params=pltpu.CompilerParams(vmem_limit_bytes=12 * MIB),
        name="tables",
    )(place, shift, flip)


def paired(re, im):
    return jnp.concatenate(
        [jnp.concatenate([re, im], 1), jnp.concatenate([im, -re], 1)], 0
    )


def halves(ref, begin):
    return paired(ref[begin : begin + BAND], ref[begin + BAND : begin + 2 * BAND])


def one_walker(up, down, cols, rows, first_up, first_down, plain, ready, put):
    step = 2 * BAND
    first_up[...] = jnp.dot(rows[: step * (TRANS + 1)], up, preferred_element_type=F32).astype(BF)
    first_down[...] = jnp.dot(rows[step:], down, preferred_element_type=F32).astype(BF)
    across = (((1,), (1,)), ((), ()))
    turned_up = lax.dot_general(rows[:step], up, across, preferred_element_type=F32).astype(BF)
    turned_down = lax.dot_general(rows[:step], down, across, preferred_element_type=F32).astype(BF)
    left = jnp.concatenate(
        [halves(turned_up, 0), halves(turned_down, 0), halves(first_up, 0)], 0
    )
    plain[...] = jnp.dot(left, cols[2 * TRANS], preferred_element_type=F32)
    ready()
    for t in range(TRANS):
        left = jnp.concatenate([halves(first_up, step * (1 + t)), halves(first_down, step * t)], 0)
        moved = jnp.dot(left, cols[t], preferred_element_type=F32)
        real, imag = 0.0, 0.0
        for s in range(2):
            nr, ni = plain[step * s : step * s + BAND], plain[step * s + BAND : step * (s + 1)]
            mr, mi = moved[step * s : step * s + BAND], moved[step * s + BAND : step * (s + 1)]
            real = real + (nr * mr + ni * mi)
            imag = imag + (nr * mi - ni * mr)
        put(0, 0, t, real)
        put(0, 1, t, imag)
        low = jnp.dot(
            halves(first_down, step * (TRANS + t)), cols[TRANS + t], preferred_element_type=F32
        )
        nr, ni = plain[2 * step : 2 * step + BAND], plain[2 * step + BAND : 3 * step]
        put(1, 0, t, nr * low[:BAND] - ni * low[BAND:])
        put(1, 1, t, nr * low[BAND:] + ni * low[:BAND])


WORK = [
    pltpu.VMEM((2 * BAND * (TRANS + 1), ORDER), BF),
    pltpu.VMEM((2 * BAND * 2 * TRANS, ORDER), BF),
    pltpu.VMEM((6 * BAND, ORDER), F32),
]
SUMS = (2, TRANS, BAND, ORDER)
PIECE = (2, ORDER, ORDER)
IN_VMEM = pl.BlockSpec(memory_space=pltpu.VMEM)
IN_SMEM = pl.BlockSpec(memory_space=pltpu.SMEM)
ANYWHERE = pl.BlockSpec(memory_space=pl.ANY)
IN_HBM = pl.BlockSpec(memory_space=pltpu.HBM)
BIG = pltpu.CompilerParams(vmem_limit_bytes=16 * MIB)


def open_kernel(
    piece, cols, rows, ph_in, pp_in, sums, kept, first_up, first_down, plain, sems
):
    loads = [
        pltpu.make_async_copy(source.at[part], sums.at[i, part], sems.at[i, part])
        for i, source in enumerate((ph_in, pp_in))
        for part in range(2)
    ]
    for load in loads:
        load.start()

    def ready():
        for load in loads:
            load.wait()

    def put(which, part, t, term):
        sums[which, part, t] += term

    one_walker(piece[0], piece[1], cols, rows.at[0], first_up, first_down, plain, ready, put)
    kept[...] = piece[...]


def open_sums(piece, cols, rows, ph, pp):
    return pl.pallas_call(
        open_kernel,
        out_shape=(jax.ShapeDtypeStruct((2, *SUMS), F32), jax.ShapeDtypeStruct(PIECE, BF)),
        in_specs=[IN_VMEM] * 3 + [IN_HBM] * 2,
        out_specs=(IN_VMEM,) * 2,
        scratch_shapes=WORK + [pltpu.SemaphoreType.DMA((2, 2))],
        cost_estimate=pl.CostEstimate(flops=4 * 10**9, bytes_accessed=1, transcendentals=0),
        compiler_params=BIG,
        name="open_sums",
    )(piece, cols, rows, ph, pp)


def spread_kernel(count, fresh, send, *refs):
    pieces = refs[:count]
    cols, rows, before = refs[count : count + 3]
    after = refs[count + 3 : count + 4 + send]
    first_up, first_down, plain, *held = refs[count + 4 + send :]
    for n, piece in enumerate(pieces):
        for b in range(2):

            def put(which, part, t, term, n=n, b=b):
                if n == 0:
                    if not (fresh and b):
                        term = term + before[2 * b + which, part, t]
                elif send and b:
                    term = term + held[0][which, part, t]
                else:
                    term = term + after[0][2 * b + which, part, t]
                if not (send and b):
                    after[0][2 * b + which, part, t] = term
                elif n < count - 1:
                    held[0][which, part, t] = term
                else:
                    after[1][which, part, t] = term.astype(BF)

            one_walker(
                piece[0], piece[1], cols, rows.at[b], first_up, first_down, plain,
                lambda: None, put,
            )


def spread(pieces, cols, rows, sums, send=False):
    count, fresh = len(pieces), sums.shape[0] == 2
    out_shape = [jax.ShapeDtypeStruct((2 if send else 4, *SUMS), F32)]
    if send:
        out_shape.append(jax.ShapeDtypeStruct((2, *SUMS), BF))
    return pl.pallas_call(
        functools.partial(spread_kernel, count, fresh, send),
        out_shape=tuple(out_shape),
        in_specs=[IN_VMEM] * (count + 3),
        out_specs=(IN_VMEM,) * len(out_shape),
        scratch_shapes=WORK + [pltpu.VMEM((2, *SUMS), F32)] * send,
        cost_estimate=TINY,
        compiler_params=BIG,
        name="spread",
    )(*pieces, cols, rows, sums)


def add_kernel(piece, cols, rows, before, after, first_up, first_down, plain):
    def put(which, part, t, term):
        after[which, part, t] = before[which, part, t] + term

    one_walker(
        piece[0], piece[1], cols, rows.at[0], first_up, first_down, plain, lambda: None, put
    )


def add(piece, cols, rows, sums):
    return pl.pallas_call(
        add_kernel,
        out_shape=jax.ShapeDtypeStruct((2, *SUMS), F32),
        in_specs=[IN_VMEM] * 4,
        out_specs=IN_VMEM,
        scratch_shapes=WORK,
        cost_estimate=TINY,
        compiler_params=BIG,
        name="add",
    )(piece, cols, rows, sums)


def close_kernel(
    piece, cols, rows, sums, others, ph, pp, first_up, first_down, plain, total, sems
):
    stores = []

    def put(which, part, t, term):
        other = others[which, part, t].astype(F32)
        total[which, part, t] = sums[which, part, t] + other + term
        store = pltpu.make_async_copy(
            total.at[which, part, t], (ph, pp)[which].at[part, t], sems.at[which, part, t]
        )
        store.start()
        stores.append(store)

    one_walker(
        piece[0], piece[1], cols, rows.at[0], first_up, first_down, plain, lambda: None, put
    )
    for store in stores:
        store.wait()


def close_sums(piece, cols, rows, sums, others):
    return pl.pallas_call(
        close_kernel,
        out_shape=(jax.ShapeDtypeStruct(SUMS, F32),) * 2,
        in_specs=[IN_VMEM] * 5,
        out_specs=(ANYWHERE,) * 2,
        scratch_shapes=WORK
        + [pltpu.VMEM((2, *SUMS), F32), pltpu.SemaphoreType.DMA((2, 2, TRANS))],
        cost_estimate=TINY,
        compiler_params=BIG,
        name="close_sums",
    )(piece, cols, rows, sums, others)


def scale_kernel(masses, spins, out):
    signed = (2 * spins[...] - 1).astype(F32)
    for spin, sign in enumerate((COUPLING, -COUPLING)):
        out[spin] = (masses[0, spin].astype(F32) * jnp.exp(sign * signed)).astype(BF)


def scale(masses, spins):
    return pl.pallas_call(
        scale_kernel,
        out_shape=jax.ShapeDtypeStruct(PIECE, BF),
        in_specs=[IN_VMEM] * 2,
        out_specs=IN_VMEM,
        cost_estimate=TINY,
        compiler_params=pltpu.CompilerParams(vmem_limit_bytes=56 * MIB),
        name="scale",
    )(masses, spins)


def route_kernel(steps, place, y_ref, own, got, *refs):
    outs, sems = refs[: len(steps)], refs[len(steps)]
    for i, step in enumerate(steps):
        wraps = (place[0] & 1 == 0) | (y_ref[0] + step >= PLANE)

        @pl.when(wraps)
        def _(i=i):
            pltpu.make_async_copy(got, outs[i], sems.at[i]).start()

        @pl.when(jnp.logical_not(wraps))
        def _(i=i):
            pltpu.make_async_copy(own, outs[i], sems.at[i]).start()

    for i in range(len(steps)):
        pltpu.make_async_copy(own, outs[i], sems.at[i]).wait()


def route(place, y, own, got, steps):
    return pl.pallas_call(
        functools.partial(route_kernel, steps),
        out_shape=(jax.ShapeDtypeStruct(own.shape, BF),) * len(steps),
        in_specs=[IN_SMEM] * 2 + [ANYWHERE] * 2,
        out_specs=(ANYWHERE,) * len(steps),
        scratch_shapes=[pltpu.SemaphoreType.DMA((len(steps),))],
        cost_estimate=TINY,
        compiler_params=pltpu.CompilerParams(vmem_limit_bytes=MIB),
        name="route",
    )(place, y, own, got)


PLANE = 4
BLOCKS = 64


def planes_back(value):
    pairs = []
    for g in range(4):
        for b in range(BLOCKS):
            target = (b + PLANE * (1 + g % 2)) % BLOCKS
            crosses = target // (BLOCKS // 2) != b // (BLOCKS // 2)
            chip = g ^ 2 if crosses else g
            pairs.append((g * BLOCKS + b, chip * BLOCKS + target))
    return lax.ppermute(value, ("grp", "blk"), pairs)


def along_y(value, steps):
    pairs = [(b, b // PLANE * PLANE + (b + steps) % PLANE) for b in range(BLOCKS)]
    return lax.ppermute(value, "blk", pairs)


def other_core(value):
    return lax.ppermute(value, "grp", [(s, s ^ 1) for s in range(4)])


def on_device(masses, spins, shift_table, flip_table, ph_in, pp_in):
    place = lax.axis_index("grp").reshape(1).astype(jnp.int32)
    y = (lax.axis_index("blk") % PLANE).reshape(1).astype(jnp.int32)
    own = scale(masses, spins)
    got = planes_back(own)
    cols, rows = tables(place, shift_table, flip_table)
    sums, kept = open_sums(own, cols, rows, ph_in, pp_in)
    right, left, middle = route(place, y, kept, got, (1, 3, 2))
    right, left = along_y(right, 1), along_y(left, 3)
    (sums,) = spread([got], cols, rows, sums)
    middle = along_y(middle, 2)
    right, sums = lax.optimization_barrier((right, sums))
    (sums,) = spread([right], cols, rows, sums)
    left, sums = lax.optimization_barrier((left, sums))
    sums, sent = spread([left], cols, rows, sums, True)
    others = other_core(sent)
    middle, sums = lax.optimization_barrier((middle, sums))
    swapped = other_core(middle)
    sums = add(middle, cols, rows, sums)
    return close_sums(swapped, cols, rows, sums, others)


def solution(mesh):
    placed = (
        P("blk", None, None, None),
        P("blk", None),
        P("blk", None),
        P("blk", None),
        P(None, "blk", "grp", None),
        P(None, "blk", "grp", None),
    )
    return jax.shard_map(
        on_device,
        mesh=mesh,
        in_specs=placed,
        out_specs=(P(None, "blk", "grp", None), P(None, "blk", "grp", None)),
        check_vma=False,
    )
```

```python
import functools
import math

import jax
import jax.numpy as jnp
from jax import lax
from jax.experimental import pallas as pl
from jax.experimental.pallas import tpu as pltpu
from jax.sharding import PartitionSpec as P

NK = 16
ORDER = 256
BAND = 64
TRANS = 4
COUPLING = 0.5
BF = jnp.bfloat16
F32 = jnp.float32
MIB = 1 << 20
TINY = pl.CostEstimate(flops=1, bytes_accessed=1, transcendentals=0)


def wave(freq, mom, tau, site):
    turns = ((2 * freq + 1) * tau - 2 * mom * site) & 31
    phase = turns.astype(F32) * (math.pi / 16.0)
    return (jnp.cos(phase) * 0.0625).astype(BF), (jnp.sin(phase) * 0.0625).astype(BF)


def table_kernel(
    place_ref, shift_in, flip_in, cols_ref, rows_ref, shift_ref, flip_ref, sems
):
    fetch = [
        pltpu.make_async_copy(shift_in, shift_ref, sems.at[0]),
        pltpu.make_async_copy(flip_in, flip_ref, sems.at[1]),
    ]
    for copy in fetch:
        copy.start()
    square = (ORDER, ORDER)
    sub = lax.broadcasted_iota(jnp.int32, square, 0)
    lane = lax.broadcasted_iota(jnp.int32, square, 1)
    re, im = wave(lane >> 4, lane & 15, sub >> 4, sub & 15)
    cols_ref[2 * TRANS, :ORDER] = re
    cols_ref[2 * TRANS, ORDER:] = im
    re, im = wave(sub >> 4, sub & 15, lane >> 4, lane & 15)
    base = jnp.concatenate([re, im], 1)
    both = lax.broadcasted_iota(jnp.int32, (2 * BAND, ORDER), 0)
    grp = jnp.where(both < BAND, place_ref[0], place_ref[0] ^ 1)
    band_row = (both & (BAND - 1)) + grp * BAND
    band_lane = lax.broadcasted_iota(jnp.int32, (2 * BAND, ORDER), 1)

    def put_rows(slot, target):
        pick = jnp.where(band_lane == target, 1.0, 0.0).astype(BF)
        out = jnp.dot(pick, base, preferred_element_type=F32).astype(BF)
        for b in range(2):
            part = out[BAND * b : BAND * (b + 1)]
            rows_ref[b, 2 * BAND * slot : 2 * BAND * slot + BAND] = part[:, :ORDER]
            rows_ref[b, 2 * BAND * slot + BAND : 2 * BAND * (slot + 1)] = part[:, ORDER:]

    def put_cols(slot, target):
        pick = jnp.where(sub == target, 1.0, 0.0).astype(BF)
        cols_ref[slot] = jnp.dot(cols_ref[2 * TRANS], pick, preferred_element_type=F32).astype(BF)

    put_rows(0, band_row)
    for copy in fetch:
        copy.wait()
    for t in range(TRANS):
        freq, mom = shift_ref[t, 0] >> 4, shift_ref[t, 0] & 15

        def moved(i, freq=freq, mom=mom):
            return ((((i >> 4) + freq) & 15) << 4) + (((i & 15) + mom) & 15)

        put_rows(1 + t, moved(band_row))
        put_cols(t, moved(lane))
        freq, mom = flip_ref[t, 0] >> 4, flip_ref[t, 0] & 15

        def turned(i, freq=freq, mom=mom):
            return (((freq - (i >> 4)) & 15) << 4) + ((mom - (i & 15)) & 15)

        put_rows(1 + TRANS + t, turned(band_row))
        put_cols(TRANS + t, turned(lane))


def tables(place, shift, flip):
    return pl.pallas_call(
        table_kernel,
        out_shape=(
            jax.ShapeDtypeStruct((2 * TRANS + 1, 2 * ORDER, ORDER), BF),
            jax.ShapeDtypeStruct((2, (2 * TRANS + 1) * 2 * BAND, ORDER), BF),
        ),
        in_specs=[
            pl.BlockSpec(memory_space=pltpu.SMEM),
            pl.BlockSpec(memory_space=pltpu.HBM),
            pl.BlockSpec(memory_space=pltpu.HBM),
        ],
        out_specs=(pl.BlockSpec(memory_space=pltpu.VMEM),) * 2,
        scratch_shapes=[
            pltpu.SMEM((TRANS, ORDER), jnp.int32),
            pltpu.SMEM((TRANS, ORDER), jnp.int32),
            pltpu.SemaphoreType.DMA((2,)),
        ],
        cost_estimate=pl.CostEstimate(flops=4 * 10**9, bytes_accessed=1, transcendentals=0),
        compiler_params=pltpu.CompilerParams(vmem_limit_bytes=12 * MIB),
        name="tables",
    )(place, shift, flip)


def paired(re, im):
    return jnp.concatenate(
        [jnp.concatenate([re, im], 1), jnp.concatenate([im, -re], 1)], 0
    )


def halves(ref, begin):
    return paired(ref[begin : begin + BAND], ref[begin + BAND : begin + 2 * BAND])


def one_walker(up, down, cols, rows, first_up, first_down, plain, ready, put):
    step = 2 * BAND
    first_up[...] = jnp.dot(rows[: step * (TRANS + 1)], up, preferred_element_type=F32).astype(BF)
    first_down[...] = jnp.dot(rows[step:], down, preferred_element_type=F32).astype(BF)
    across = (((1,), (1,)), ((), ()))
    turned_up = lax.dot_general(rows[:step], up, across, preferred_element_type=F32).astype(BF)
    turned_down = lax.dot_general(rows[:step], down, across, preferred_element_type=F32).astype(BF)
    left = jnp.concatenate(
        [halves(turned_up, 0), halves(turned_down, 0), halves(first_up, 0)], 0
    )
    plain[...] = jnp.dot(left, cols[2 * TRANS], preferred_element_type=F32)
    ready()
    for t in range(TRANS):
        left = jnp.concatenate([halves(first_up, step * (1 + t)), halves(first_down, step * t)], 0)
        moved = jnp.dot(left, cols[t], preferred_element_type=F32)
        real, imag = 0.0, 0.0
        for s in range(2):
            nr, ni = plain[step * s : step * s + BAND], plain[step * s + BAND : step * (s + 1)]
            mr, mi = moved[step * s : step * s + BAND], moved[step * s + BAND : step * (s + 1)]
            real = real + (nr * mr + ni * mi)
            imag = imag + (nr * mi - ni * mr)
        put(0, 0, t, real)
        put(0, 1, t, imag)
        low = jnp.dot(
            halves(first_down, step * (TRANS + t)), cols[TRANS + t], preferred_element_type=F32
        )
        nr, ni = plain[2 * step : 2 * step + BAND], plain[2 * step + BAND : 3 * step]
        put(1, 0, t, nr * low[:BAND] - ni * low[BAND:])
        put(1, 1, t, nr * low[BAND:] + ni * low[:BAND])


WORK = [
    pltpu.VMEM((2 * BAND * (TRANS + 1), ORDER), BF),
    pltpu.VMEM((2 * BAND * 2 * TRANS, ORDER), BF),
    pltpu.VMEM((6 * BAND, ORDER), F32),
]
SUMS = (2, TRANS, BAND, ORDER)
PIECE = (2, ORDER, ORDER)
IN_VMEM = pl.BlockSpec(memory_space=pltpu.VMEM)
IN_SMEM = pl.BlockSpec(memory_space=pltpu.SMEM)
ANYWHERE = pl.BlockSpec(memory_space=pl.ANY)
IN_HBM = pl.BlockSpec(memory_space=pltpu.HBM)
BIG = pltpu.CompilerParams(vmem_limit_bytes=16 * MIB)


def open_kernel(
    piece, cols, rows, ph_in, pp_in, sums, kept, first_up, first_down, plain, sems
):
    loads = [
        pltpu.make_async_copy(source.at[part], sums.at[i, part], sems.at[i, part])
        for i, source in enumerate((ph_in, pp_in))
        for part in range(2)
    ]
    for load in loads:
        load.start()

    def ready():
        for load in loads:
            load.wait()

    def put(which, part, t, term):
        sums[which, part, t] += term

    one_walker(piece[0], piece[1], cols, rows.at[0], first_up, first_down, plain, ready, put)
    kept[...] = piece[...]


def open_sums(piece, cols, rows, ph, pp):
    return pl.pallas_call(
        open_kernel,
        out_shape=(jax.ShapeDtypeStruct((2, *SUMS), F32), jax.ShapeDtypeStruct(PIECE, BF)),
        in_specs=[IN_VMEM] * 3 + [IN_HBM] * 2,
        out_specs=(IN_VMEM,) * 2,
        scratch_shapes=WORK + [pltpu.SemaphoreType.DMA((2, 2))],
        cost_estimate=pl.CostEstimate(flops=4 * 10**9, bytes_accessed=1, transcendentals=0),
        compiler_params=BIG,
        name="open_sums",
    )(piece, cols, rows, ph, pp)


def spread_kernel(count, fresh, send, *refs):
    pieces = refs[:count]
    cols, rows, before = refs[count : count + 3]
    after = refs[count + 3 : count + 4 + send]
    first_up, first_down, plain, *held = refs[count + 4 + send :]
    for n, piece in enumerate(pieces):
        for b in range(2):

            def put(which, part, t, term, n=n, b=b):
                if n == 0:
                    if not (fresh and b):
                        term = term + before[2 * b + which, part, t]
                elif send and b:
                    term = term + held[0][which, part, t]
                else:
                    term = term + after[0][2 * b + which, part, t]
                if not (send and b):
                    after[0][2 * b + which, part, t] = term
                elif n < count - 1:
                    held[0][which, part, t] = term
                else:
                    after[1][which, part, t] = term.astype(BF)

            one_walker(
                piece[0], piece[1], cols, rows.at[b], first_up, first_down, plain,
                lambda: None, put,
            )


def spread(pieces, cols, rows, sums, send=False):
    count, fresh = len(pieces), sums.shape[0] == 2
    out_shape = [jax.ShapeDtypeStruct((2 if send else 4, *SUMS), F32)]
    if send:
        out_shape.append(jax.ShapeDtypeStruct((2, *SUMS), BF))
    return pl.pallas_call(
        functools.partial(spread_kernel, count, fresh, send),
        out_shape=tuple(out_shape),
        in_specs=[IN_VMEM] * (count + 3),
        out_specs=(IN_VMEM,) * len(out_shape),
        scratch_shapes=WORK + [pltpu.VMEM((2, *SUMS), F32)] * send,
        cost_estimate=TINY,
        compiler_params=BIG,
        name="spread",
    )(*pieces, cols, rows, sums)


def add_kernel(piece, cols, rows, before, after, first_up, first_down, plain):
    def put(which, part, t, term):
        after[which, part, t] = before[which, part, t] + term

    one_walker(
        piece[0], piece[1], cols, rows.at[0], first_up, first_down, plain, lambda: None, put
    )


def add(piece, cols, rows, sums):
    return pl.pallas_call(
        add_kernel,
        out_shape=jax.ShapeDtypeStruct((2, *SUMS), F32),
        in_specs=[IN_VMEM] * 4,
        out_specs=IN_VMEM,
        scratch_shapes=WORK,
        cost_estimate=TINY,
        compiler_params=BIG,
        name="add",
    )(piece, cols, rows, sums)


def close_kernel(
    piece, cols, rows, sums, others, ph, pp, first_up, first_down, plain, total, sems
):
    stores = []

    def put(which, part, t, term):
        other = others[which, part, t].astype(F32)
        total[which, part, t] = sums[which, part, t] + other + term
        store = pltpu.make_async_copy(
            total.at[which, part, t], (ph, pp)[which].at[part, t], sems.at[which, part, t]
        )
        store.start()
        stores.append(store)

    one_walker(
        piece[0], piece[1], cols, rows.at[0], first_up, first_down, plain, lambda: None, put
    )
    for store in stores:
        store.wait()


def close_sums(piece, cols, rows, sums, others):
    return pl.pallas_call(
        close_kernel,
        out_shape=(jax.ShapeDtypeStruct(SUMS, F32),) * 2,
        in_specs=[IN_VMEM] * 5,
        out_specs=(ANYWHERE,) * 2,
        scratch_shapes=WORK
        + [pltpu.VMEM((2, *SUMS), F32), pltpu.SemaphoreType.DMA((2, 2, TRANS))],
        cost_estimate=TINY,
        compiler_params=BIG,
        name="close_sums",
    )(piece, cols, rows, sums, others)


def scale_kernel(masses, spins, out):
    signed = (2 * spins[...] - 1).astype(F32)
    for spin, sign in enumerate((COUPLING, -COUPLING)):
        out[spin] = (masses[0, spin].astype(F32) * jnp.exp(sign * signed)).astype(BF)


def scale(masses, spins):
    return pl.pallas_call(
        scale_kernel,
        out_shape=jax.ShapeDtypeStruct(PIECE, BF),
        in_specs=[IN_VMEM] * 2,
        out_specs=IN_VMEM,
        cost_estimate=TINY,
        compiler_params=pltpu.CompilerParams(vmem_limit_bytes=56 * MIB),
        name="scale",
    )(masses, spins)


def route_kernel(steps, place, y_ref, own, got, *refs):
    outs, sems = refs[: len(steps)], refs[len(steps)]
    for i, step in enumerate(steps):
        wraps = (place[0] & 1 == 0) | (y_ref[0] + step >= PLANE)

        @pl.when(wraps)
        def _(i=i):
            pltpu.make_async_copy(got, outs[i], sems.at[i]).start()

        @pl.when(jnp.logical_not(wraps))
        def _(i=i):
            pltpu.make_async_copy(own, outs[i], sems.at[i]).start()

    for i in range(len(steps)):
        pltpu.make_async_copy(own, outs[i], sems.at[i]).wait()


def route(place, y, own, got, steps):
    return pl.pallas_call(
        functools.partial(route_kernel, steps),
        out_shape=(jax.ShapeDtypeStruct(own.shape, BF),) * len(steps),
        in_specs=[IN_SMEM] * 2 + [ANYWHERE] * 2,
        out_specs=(ANYWHERE,) * len(steps),
        scratch_shapes=[pltpu.SemaphoreType.DMA((len(steps),))],
        cost_estimate=TINY,
        compiler_params=pltpu.CompilerParams(vmem_limit_bytes=MIB),
        name="route",
    )(place, y, own, got)


PLANE = 4
BLOCKS = 64


def planes_back(value):
    pairs = []
    for g in range(4):
        for b in range(BLOCKS):
            target = (b + PLANE * (1 + g % 2)) % BLOCKS
            crosses = target // (BLOCKS // 2) != b // (BLOCKS // 2)
            chip = g ^ 2 if crosses else g
            pairs.append((g * BLOCKS + b, chip * BLOCKS + target))
    return lax.ppermute(value, ("grp", "blk"), pairs)


def along_y(value, steps):
    pairs = [
        (g * BLOCKS + b, g * BLOCKS + b // PLANE * PLANE + (b + steps[g % 2]) % PLANE)
        for g in range(4)
        for b in range(BLOCKS)
    ]
    return lax.ppermute(value, ("grp", "blk"), pairs)


def other_core(value):
    return lax.ppermute(value, "grp", [(s, s ^ 1) for s in range(4)])


def on_device(masses, spins, shift_table, flip_table, ph_in, pp_in):
    place = lax.axis_index("grp").reshape(1).astype(jnp.int32)
    y = (lax.axis_index("blk") % PLANE).reshape(1).astype(jnp.int32)
    own = scale(masses, spins)
    got = planes_back(own)
    cols, rows = tables(place, shift_table, flip_table)
    sums, kept = open_sums(own, cols, rows, ph_in, pp_in)
    right, left, middle = route(place, y, kept, got, (3, 1, 2))
    right, left = along_y(right, (1, 3)), along_y(left, (3, 1))
    (sums,) = spread([got], cols, rows, sums)
    middle, sums = lax.optimization_barrier((middle, sums))
    middle = along_y(middle, (2, 2))
    right, sums = lax.optimization_barrier((right, sums))
    (sums,) = spread([right], cols, rows, sums)
    left, sums = lax.optimization_barrier((left, sums))
    sums, sent = spread([left], cols, rows, sums, True)
    others = other_core(sent)
    middle, sums = lax.optimization_barrier((middle, sums))
    swapped = other_core(middle)
    sums = add(middle, cols, rows, sums)
    return close_sums(swapped, cols, rows, sums, others)


def solution(mesh):
    placed = (
        P("blk", None, None, None),
        P("blk", None),
        P("blk", None),
        P("blk", None),
        P(None, "blk", "grp", None),
        P(None, "blk", "grp", None),
    )
    return jax.shard_map(
        on_device,
        mesh=mesh,
        in_specs=placed,
        out_specs=(P(None, "blk", "grp", None), P(None, "blk", "grp", None)),
        check_vma=False,
    )
```

```python
import functools
import math

import jax
import jax.numpy as jnp
from jax import lax
from jax.experimental import pallas as pl
from jax.experimental.pallas import tpu as pltpu
from jax.sharding import PartitionSpec as P

NK = 16
ORDER = 256
BAND = 64
TRANS = 4
COUPLING = 0.5
BF = jnp.bfloat16
F32 = jnp.float32
MIB = 1 << 20
TINY = pl.CostEstimate(flops=1, bytes_accessed=1, transcendentals=0)


def wave(freq, mom, tau, site):
    turns = ((2 * freq + 1) * tau - 2 * mom * site) & 31
    phase = turns.astype(F32) * (math.pi / 16.0)
    return (jnp.cos(phase) * 0.0625).astype(BF), (jnp.sin(phase) * 0.0625).astype(BF)


def table_kernel(
    place_ref, shift_in, flip_in, cols_ref, rows_ref, shift_ref, flip_ref, sems
):
    fetch = [
        pltpu.make_async_copy(shift_in, shift_ref, sems.at[0]),
        pltpu.make_async_copy(flip_in, flip_ref, sems.at[1]),
    ]
    for copy in fetch:
        copy.start()
    square = (ORDER, ORDER)
    sub = lax.broadcasted_iota(jnp.int32, square, 0)
    lane = lax.broadcasted_iota(jnp.int32, square, 1)
    re, im = wave(lane >> 4, lane & 15, sub >> 4, sub & 15)
    cols_ref[2 * TRANS, :ORDER] = re
    cols_ref[2 * TRANS, ORDER:] = im
    re, im = wave(sub >> 4, sub & 15, lane >> 4, lane & 15)
    base = jnp.concatenate([re, im], 1)
    both = lax.broadcasted_iota(jnp.int32, (2 * BAND, ORDER), 0)
    grp = jnp.where(both < BAND, place_ref[0], place_ref[0] ^ 1)
    band_row = (both & (BAND - 1)) + grp * BAND
    band_lane = lax.broadcasted_iota(jnp.int32, (2 * BAND, ORDER), 1)

    def put_rows(slot, target):
        pick = jnp.where(band_lane == target, 1.0, 0.0).astype(BF)
        out = jnp.dot(pick, base, preferred_element_type=F32).astype(BF)
        for b in range(2):
            part = out[BAND * b : BAND * (b + 1)]
            rows_ref[b, 2 * BAND * slot : 2 * BAND * slot + BAND] = part[:, :ORDER]
            rows_ref[b, 2 * BAND * slot + BAND : 2 * BAND * (slot + 1)] = part[:, ORDER:]

    def put_cols(slot, target):
        pick = jnp.where(sub == target, 1.0, 0.0).astype(BF)
        cols_ref[slot] = jnp.dot(cols_ref[2 * TRANS], pick, preferred_element_type=F32).astype(BF)

    put_rows(0, band_row)
    for copy in fetch:
        copy.wait()
    for t in range(TRANS):
        freq, mom = shift_ref[t, 0] >> 4, shift_ref[t, 0] & 15

        def moved(i, freq=freq, mom=mom):
            return ((((i >> 4) + freq) & 15) << 4) + (((i & 15) + mom) & 15)

        put_rows(1 + t, moved(band_row))
        put_cols(t, moved(lane))
        freq, mom = flip_ref[t, 0] >> 4, flip_ref[t, 0] & 15

        def turned(i, freq=freq, mom=mom):
            return (((freq - (i >> 4)) & 15) << 4) + ((mom - (i & 15)) & 15)

        put_rows(1 + TRANS + t, turned(band_row))
        put_cols(TRANS + t, turned(lane))


def tables(place, shift, flip):
    return pl.pallas_call(
        table_kernel,
        out_shape=(
            jax.ShapeDtypeStruct((2 * TRANS + 1, 2 * ORDER, ORDER), BF),
            jax.ShapeDtypeStruct((2, (2 * TRANS + 1) * 2 * BAND, ORDER), BF),
        ),
        in_specs=[
            pl.BlockSpec(memory_space=pltpu.SMEM),
            pl.BlockSpec(memory_space=pltpu.HBM),
            pl.BlockSpec(memory_space=pltpu.HBM),
        ],
        out_specs=(pl.BlockSpec(memory_space=pltpu.VMEM),) * 2,
        scratch_shapes=[
            pltpu.SMEM((TRANS, ORDER), jnp.int32),
            pltpu.SMEM((TRANS, ORDER), jnp.int32),
            pltpu.SemaphoreType.DMA((2,)),
        ],
        cost_estimate=pl.CostEstimate(flops=4 * 10**9, bytes_accessed=1, transcendentals=0),
        compiler_params=pltpu.CompilerParams(vmem_limit_bytes=12 * MIB),
        name="tables",
    )(place, shift, flip)


def paired(re, im):
    return jnp.concatenate(
        [jnp.concatenate([re, im], 1), jnp.concatenate([im, -re], 1)], 0
    )


def halves(ref, begin):
    return paired(ref[begin : begin + BAND], ref[begin + BAND : begin + 2 * BAND])


def one_walker(up, down, cols, rows, first_up, first_down, plain, ready, put):
    step = 2 * BAND
    first_up[...] = jnp.dot(rows[: step * (TRANS + 1)], up, preferred_element_type=F32).astype(BF)
    first_down[...] = jnp.dot(rows[step:], down, preferred_element_type=F32).astype(BF)
    across = (((1,), (1,)), ((), ()))
    turned_up = lax.dot_general(rows[:step], up, across, preferred_element_type=F32).astype(BF)
    turned_down = lax.dot_general(rows[:step], down, across, preferred_element_type=F32).astype(BF)
    left = jnp.concatenate(
        [halves(turned_up, 0), halves(turned_down, 0), halves(first_up, 0)], 0
    )
    plain[...] = jnp.dot(left, cols[2 * TRANS], preferred_element_type=F32)
    ready()
    for t in range(TRANS):
        left = jnp.concatenate([halves(first_up, step * (1 + t)), halves(first_down, step * t)], 0)
        moved = jnp.dot(left, cols[t], preferred_element_type=F32)
        real, imag = 0.0, 0.0
        for s in range(2):
            nr, ni = plain[step * s : step * s + BAND], plain[step * s + BAND : step * (s + 1)]
            mr, mi = moved[step * s : step * s + BAND], moved[step * s + BAND : step * (s + 1)]
            real = real + (nr * mr + ni * mi)
            imag = imag + (nr * mi - ni * mr)
        put(0, 0, t, real)
        put(0, 1, t, imag)
        low = jnp.dot(
            halves(first_down, step * (TRANS + t)), cols[TRANS + t], preferred_element_type=F32
        )
        nr, ni = plain[2 * step : 2 * step + BAND], plain[2 * step + BAND : 3 * step]
        put(1, 0, t, nr * low[:BAND] - ni * low[BAND:])
        put(1, 1, t, nr * low[BAND:] + ni * low[:BAND])


WORK = [
    pltpu.VMEM((2 * BAND * (TRANS + 1), ORDER), BF),
    pltpu.VMEM((2 * BAND * 2 * TRANS, ORDER), BF),
    pltpu.VMEM((6 * BAND, ORDER), F32),
]
SUMS = (2, TRANS, BAND, ORDER)
PIECE = (2, ORDER, ORDER)
IN_VMEM = pl.BlockSpec(memory_space=pltpu.VMEM)
IN_SMEM = pl.BlockSpec(memory_space=pltpu.SMEM)
ANYWHERE = pl.BlockSpec(memory_space=pl.ANY)
IN_HBM = pl.BlockSpec(memory_space=pltpu.HBM)
BIG = pltpu.CompilerParams(vmem_limit_bytes=16 * MIB)


def open_kernel(
    piece, cols, rows, ph_in, pp_in, sums, kept, first_up, first_down, plain, sems
):
    loads = [
        pltpu.make_async_copy(source.at[part], sums.at[i, part], sems.at[i, part])
        for i, source in enumerate((ph_in, pp_in))
        for part in range(2)
    ]
    for load in loads:
        load.start()

    def ready():
        for load in loads:
            load.wait()

    def put(which, part, t, term):
        sums[which, part, t] += term

    one_walker(piece[0], piece[1], cols, rows.at[0], first_up, first_down, plain, ready, put)
    kept[...] = piece[...]


def open_sums(piece, cols, rows, ph, pp):
    return pl.pallas_call(
        open_kernel,
        out_shape=(jax.ShapeDtypeStruct((2, *SUMS), F32), jax.ShapeDtypeStruct(PIECE, BF)),
        in_specs=[IN_VMEM] * 3 + [IN_HBM] * 2,
        out_specs=(IN_VMEM,) * 2,
        scratch_shapes=WORK + [pltpu.SemaphoreType.DMA((2, 2))],
        cost_estimate=pl.CostEstimate(flops=4 * 10**9, bytes_accessed=1, transcendentals=0),
        compiler_params=BIG,
        name="open_sums",
    )(piece, cols, rows, ph, pp)


def spread_kernel(count, fresh, send, *refs):
    pieces = refs[:count]
    cols, rows, before = refs[count : count + 3]
    after = refs[count + 3 : count + 4 + send]
    first_up, first_down, plain, *held = refs[count + 4 + send :]
    for n, piece in enumerate(pieces):
        for b in range(2):

            def put(which, part, t, term, n=n, b=b):
                if n == 0:
                    if not (fresh and b):
                        term = term + before[2 * b + which, part, t]
                elif send and b:
                    term = term + held[0][which, part, t]
                else:
                    term = term + after[0][2 * b + which, part, t]
                if not (send and b):
                    after[0][2 * b + which, part, t] = term
                elif n < count - 1:
                    held[0][which, part, t] = term
                else:
                    after[1][which, part, t] = term.astype(BF)

            one_walker(
                piece[0], piece[1], cols, rows.at[b], first_up, first_down, plain,
                lambda: None, put,
            )


def spread(pieces, cols, rows, sums, send=False):
    count, fresh = len(pieces), sums.shape[0] == 2
    out_shape = [jax.ShapeDtypeStruct((2 if send else 4, *SUMS), F32)]
    if send:
        out_shape.append(jax.ShapeDtypeStruct((2, *SUMS), BF))
    return pl.pallas_call(
        functools.partial(spread_kernel, count, fresh, send),
        out_shape=tuple(out_shape),
        in_specs=[IN_VMEM] * (count + 3),
        out_specs=(IN_VMEM,) * len(out_shape),
        scratch_shapes=WORK + [pltpu.VMEM((2, *SUMS), F32)] * send,
        cost_estimate=TINY,
        compiler_params=BIG,
        name="spread",
    )(*pieces, cols, rows, sums)


def add_kernel(piece, cols, rows, before, after, first_up, first_down, plain):
    def put(which, part, t, term):
        after[which, part, t] = before[which, part, t] + term

    one_walker(
        piece[0], piece[1], cols, rows.at[0], first_up, first_down, plain, lambda: None, put
    )


def add(piece, cols, rows, sums):
    return pl.pallas_call(
        add_kernel,
        out_shape=jax.ShapeDtypeStruct((2, *SUMS), F32),
        in_specs=[IN_VMEM] * 4,
        out_specs=IN_VMEM,
        scratch_shapes=WORK,
        cost_estimate=TINY,
        compiler_params=BIG,
        name="add",
    )(piece, cols, rows, sums)


def close_kernel(
    piece, cols, rows, sums, others, ph, pp, first_up, first_down, plain, total, sems
):
    stores = []

    def put(which, part, t, term):
        other = others[which, part, t].astype(F32)
        total[which, part, t] = sums[which, part, t] + other + term
        store = pltpu.make_async_copy(
            total.at[which, part, t], (ph, pp)[which].at[part, t], sems.at[which, part, t]
        )
        store.start()
        stores.append(store)

    one_walker(
        piece[0], piece[1], cols, rows.at[0], first_up, first_down, plain, lambda: None, put
    )
    for store in stores:
        store.wait()


def close_sums(piece, cols, rows, sums, others):
    return pl.pallas_call(
        close_kernel,
        out_shape=(jax.ShapeDtypeStruct(SUMS, F32),) * 2,
        in_specs=[IN_VMEM] * 5,
        out_specs=(ANYWHERE,) * 2,
        scratch_shapes=WORK
        + [pltpu.VMEM((2, *SUMS), F32), pltpu.SemaphoreType.DMA((2, 2, TRANS))],
        cost_estimate=TINY,
        compiler_params=BIG,
        name="close_sums",
    )(piece, cols, rows, sums, others)


def scale_kernel(masses, spins, out, raw, done, sems):
    loads = [pltpu.make_async_copy(masses.at[0, s], raw.at[s], sems.at[0, s]) for s in range(2)]
    stores = [pltpu.make_async_copy(done.at[s], out.at[s], sems.at[1, s]) for s in range(2)]
    for load in loads:
        load.start()
    signed = (2 * spins[...] - 1).astype(F32)
    for s, sign in enumerate((COUPLING, -COUPLING)):
        loads[s].wait()
        done[s] = (raw[s].astype(F32) * jnp.exp(sign * signed)).astype(BF)
        stores[s].start()
    for store in stores:
        store.wait()


def scale(masses, spins):
    return pl.pallas_call(
        scale_kernel,
        out_shape=jax.ShapeDtypeStruct(PIECE, BF),
        in_specs=[ANYWHERE, IN_VMEM],
        out_specs=ANYWHERE,
        scratch_shapes=[pltpu.VMEM(PIECE, BF)] * 2 + [pltpu.SemaphoreType.DMA((2, 2))],
        cost_estimate=TINY,
        compiler_params=pltpu.CompilerParams(vmem_limit_bytes=56 * MIB),
        name="scale",
    )(masses, spins)


def route_kernel(steps, place, y_ref, own, got, *refs):
    outs, sems = refs[: len(steps)], refs[len(steps)]
    for i, step in enumerate(steps):
        wraps = (place[0] & 1 == 0) | (y_ref[0] + step >= PLANE)

        @pl.when(wraps)
        def _(i=i):
            pltpu.make_async_copy(got, outs[i], sems.at[i]).start()

        @pl.when(jnp.logical_not(wraps))
        def _(i=i):
            pltpu.make_async_copy(own, outs[i], sems.at[i]).start()

    for i in range(len(steps)):
        pltpu.make_async_copy(own, outs[i], sems.at[i]).wait()


def route(place, y, own, got, steps):
    return pl.pallas_call(
        functools.partial(route_kernel, steps),
        out_shape=(jax.ShapeDtypeStruct(own.shape, BF),) * len(steps),
        in_specs=[IN_SMEM] * 2 + [ANYWHERE] * 2,
        out_specs=(ANYWHERE,) * len(steps),
        scratch_shapes=[pltpu.SemaphoreType.DMA((len(steps),))],
        cost_estimate=TINY,
        compiler_params=pltpu.CompilerParams(vmem_limit_bytes=MIB),
        name="route",
    )(place, y, own, got)


PLANE = 4
BLOCKS = 64


def planes_back(value):
    pairs = []
    for g in range(4):
        for b in range(BLOCKS):
            target = (b + PLANE * (1 + g % 2)) % BLOCKS
            crosses = target // (BLOCKS // 2) != b // (BLOCKS // 2)
            chip = g ^ 2 if crosses else g
            pairs.append((g * BLOCKS + b, chip * BLOCKS + target))
    return lax.ppermute(value, ("grp", "blk"), pairs)


def along_y(value, steps):
    pairs = [(b, b // PLANE * PLANE + (b + steps) % PLANE) for b in range(BLOCKS)]
    return lax.ppermute(value, "blk", pairs)


def other_core(value):
    return lax.ppermute(value, "grp", [(s, s ^ 1) for s in range(4)])


def on_device(masses, spins, shift_table, flip_table, ph_in, pp_in):
    place = lax.axis_index("grp").reshape(1).astype(jnp.int32)
    y = (lax.axis_index("blk") % PLANE).reshape(1).astype(jnp.int32)
    own = scale(masses, spins)
    got = planes_back(own)
    cols, rows = tables(place, shift_table, flip_table)
    sums, kept = open_sums(own, cols, rows, ph_in, pp_in)
    right, left, middle = route(place, y, kept, got, (1, 3, 2))
    right, left = along_y(right, 1), along_y(left, 3)
    (sums,) = spread([got], cols, rows, sums)
    middle, sums = lax.optimization_barrier((middle, sums))
    middle = along_y(middle, 2)
    right, sums = lax.optimization_barrier((right, sums))
    (sums,) = spread([right], cols, rows, sums)
    left, sums = lax.optimization_barrier((left, sums))
    sums, sent = spread([left], cols, rows, sums, True)
    others = other_core(sent)
    middle, sums = lax.optimization_barrier((middle, sums))
    swapped = other_core(middle)
    sums = add(middle, cols, rows, sums)
    return close_sums(swapped, cols, rows, sums, others)


def solution(mesh):
    placed = (
        P("blk", None, None, None),
        P("blk", None),
        P("blk", None),
        P("blk", None),
        P(None, "blk", "grp", None),
        P(None, "blk", "grp", None),
    )
    return jax.shard_map(
        on_device,
        mesh=mesh,
        in_specs=placed,
        out_specs=(P(None, "blk", "grp", None), P(None, "blk", "grp", None)),
        check_vma=False,
    )
```
